128 devices in a mesh: dom: 8 (over y, core), col: 16 (over z, x).
Axes of the slice: x: 4, y: 4, z: 4, core: 2. Of those that a mesh axis runs over, the one named last changes fastest.
Arguments:
- orbitals: bfloat16 [128, 16, 128, 1024], P(('dom', 'col')), may hold values from -1 to 1
- potential: float32 [128, 1024], P(('dom', 'col')), may hold values from -6 to 6
- domain_start: int32 [128], P(('dom', 'col')), may hold values from 0 to 31
- margin_pairs: int32 [128, 2, 228], P(('dom', 'col')), may hold values from 0 to 15, as said below
- coefficients: bfloat16 [4, 8, 128, 16, 128], P(None, 'dom', None, 'col'), may hold values from -0.25 to 0.25
Outputs:
- potential_blocks: bfloat16 [4, 8, 2, 16, 128, 128], P(None, 'dom', None, 'col')
- product: float32 [2, 16, 128, 16, 128], P(None, 'col', None, 'dom')
The draws below stay inside these ranges and needn't reach their ends.
Inputs may be any that keep to these rules, and one draw needn't show every extreme that they name: `margin_pairs`: each domain lists 228 distinct ordered pairs; if (a, b) is listed so is (b, a); every pair with |a - b| <= 8 is listed.
All inputs are finite; a program needn't handle non-finite values.
Results may differ from the reference program's by a relative error of at most 0.0057.
Values may be sent and summed in bfloat16 or wider, within the bound.
No kernel may reach another device: no remote copies, remote signals or barrier semaphores. Data moves between devices by JAX's collectives and lax.ppermute only.
A program may use at most 128 MiB of HBM per device.

```python
import jax
import jax.numpy as jnp
import numpy as np
from jax import lax

NB = 128
LOC = 16
G_DEV = 1024
DOMAINS = 128
NBLK = 32
CB = 4
CC = 2
KPC = 64
PAIRS = 228
N_DOM = 8
N_COL = 16


def draw_domain_start(key, part):
    key = jax.random.fold_in(key, 5)
    first_key, second_key = jax.random.split(key)
    starts = jax.random.randint(first_key, (DOMAINS,), 0, NBLK)
    shuffle = jax.random.permutation(second_key, DOMAINS)
    starts = starts.at[shuffle[0]].set(NBLK - 1)
    starts = starts.at[shuffle[1]].set(0)
    return starts.astype(jnp.int32)


def draw_margin_pairs(key, part):
    key = jax.random.fold_in(key, 9)
    reach = LOC // 2
    near_pairs = np.array([[lower_idx, upper_idx] for lower_idx in range(LOC) for upper_idx in range(lower_idx + 1, LOC) if upper_idx - lower_idx <= reach], np.int32)
    far_pairs = np.array([[lower_idx, upper_idx] for lower_idx in range(LOC) for upper_idx in range(lower_idx + 1, LOC) if upper_idx - lower_idx > reach], np.int32).reshape(-1, 2)
    diagonal = np.array([[lower_idx, lower_idx] for lower_idx in range(LOC)], np.int32)
    keep_count = far_pairs.shape[0] // 2
    first_key, second_key = jax.random.split(key)
    choose_keys = jax.random.split(first_key, DOMAINS)
    shuffle_keys = jax.random.split(second_key, DOMAINS)
    fixed_part = np.concatenate([diagonal, near_pairs, near_pairs[:, ::-1]], axis=0)
    fixed_part = jnp.broadcast_to(jnp.asarray(fixed_part), (DOMAINS,) + fixed_part.shape)
    if keep_count > 0:
        chosen_index = jax.vmap(lambda subkey: jax.random.permutation(subkey, far_pairs.shape[0])[:keep_count])(choose_keys)
        chosen = jnp.asarray(far_pairs)[chosen_index]
        listed = jnp.concatenate([fixed_part, chosen, chosen[:, :, ::-1]], axis=1)
    else:
        listed = fixed_part
    shuffle = jax.vmap(lambda subkey: jax.random.permutation(subkey, PAIRS))(shuffle_keys)
    listed = jnp.take_along_axis(listed, shuffle[:, :, None], axis=1)
    return jnp.transpose(listed, (0, 2, 1)).astype(jnp.int32)


def block_scale(own_key, shape, cuts, low, top_value):
    def one(position, shards_of):
        draws = jax.random.uniform(jax.random.fold_in(jax.random.fold_in(own_key, 6), position), (shards_of,), jnp.float32, low / len(cuts), top_value / len(cuts))
        return jnp.repeat(jnp.exp(draws), shape[position] // shards_of).reshape((-1,) + (1,) * (len(shape) - position - 1))

    factor_of = one(*cuts[0])
    for cut in cuts[1:]:
        factor_of = factor_of * one(*cut)
    return factor_of


def normal_values(key, shape, scale, bound, shards=(), kind=jnp.bfloat16):
    gain = block_scale(key, shape, shards, -0.22, 0.18) if shards else 1.0
    values = jax.random.normal(key, shape, jnp.float32) * scale * gain
    return jnp.minimum(jnp.maximum(values, -bound), bound).astype(kind)


def setup_inputs(seed: int = 0) -> dict:
    splits = jax.random.split(jax.random.key(seed), 6)
    orbitals = normal_values(splits[0], (DOMAINS, LOC, NB, G_DEV), ((4 * LOC * G_DEV) ** -0.25), 1.0, ((0, 128),))
    potential = normal_values(splits[1], (DOMAINS, G_DEV), 1.0, 6.0, ((0, 128),), jnp.float32)
    domain_start = draw_domain_start(jax.random.fold_in(splits[5], 71), 0)
    margin_pairs = draw_margin_pairs(jax.random.fold_in(splits[5], 71), 0)
    coefficients = normal_values(splits[4], (CB, N_DOM, NB, N_COL, 2 * KPC), ((2 * LOC * NB) ** -0.5), 0.25, ((1, 8), (3, 16)))
    return dict(orbitals=orbitals, potential=potential, domain_start=domain_start, margin_pairs=margin_pairs, coefficients=coefficients)


def reference(orbitals, potential, domain_start, margin_pairs, coefficients):
    def add_domain(running, domain_items):
        basis_values, local_potential, first_block, pair_list = domain_items
        weighted = (basis_values.astype(jnp.float32) * local_potential[None, None, :]).astype(jnp.bfloat16)
        left_side = weighted.astype(jnp.float32).reshape(LOC * NB, G_DEV)
        right_side = basis_values.astype(jnp.float32).reshape(LOC * NB, G_DEV)
        dense_blocks = jnp.dot(left_side, right_side.T, precision=lax.Precision.HIGHEST).reshape(LOC, NB, LOC, NB)
        pair_rows = pair_list[0]
        pair_cols = pair_list[1]
        picked = dense_blocks[pair_rows, :, pair_cols, :]
        picked = lax.optimization_barrier(picked.astype(jnp.bfloat16)).astype(jnp.float32)
        row_block = ((first_block + pair_rows) % NBLK).astype(jnp.int32)
        col_block = ((first_block + pair_cols) % NBLK).astype(jnp.int32)
        running = running.at[row_block, col_block].add(picked)
        return running, None

    initial = jnp.zeros((NBLK, NBLK, NB, NB), jnp.float32)
    running, _ = lax.scan(add_domain, initial, (orbitals, potential, domain_start, margin_pairs))
    blocks = running.astype(jnp.bfloat16)
    potential_blocks = blocks.reshape(CB, N_DOM, CC, N_COL, NB, NB)
    panel = coefficients.astype(jnp.float32).reshape(NBLK, NB, N_COL * 2 * KPC)
    applied = jnp.einsum("IJij,Iim->Jjm", blocks.astype(jnp.float32), panel, precision=lax.Precision.HIGHEST)
    product = applied.reshape(CC, N_COL, NB, N_COL, 2 * KPC)
    return potential_blocks, product
```

```python
import functools

import jax
import jax.numpy as jnp
from jax import lax
from jax.experimental import pallas as pl
from jax.experimental.pallas import tpu as pltpu
from jax.sharding import PartitionSpec as P

F32 = jnp.float32
BF16 = jnp.bfloat16
AXES = ("dom", "col")
NB = 128
LOC = 16
NBLK = 32
NDOM = 8
NCOL = 16
NDEV = NDOM * NCOL
ROWS = NB + 8
HELD = 4 * NB + 16
CHUNK = 8
VMEM = pl.BlockSpec(memory_space=pltpu.VMEM)
SMEM = pl.BlockSpec(memory_space=pltpu.SMEM)


def upper(strict):
    row = lax.broadcasted_iota(jnp.int32, (NB, NB), 0)
    col = lax.broadcasted_iota(jnp.int32, (NB, NB), 1)
    return row < col if strict else row <= col


def message_kernel(start_ref, pairs_ref, potential_ref, orbitals_ref, out_ref, held, weighted, diagonal, sems):
    step_rows = 2 * NB
    steps = LOC // 2
    copies = [
        pltpu.make_async_copy(
            orbitals_ref.at[pl.ds(k * step_rows, step_rows)], held.at[pl.ds(k * step_rows, step_rows)], sems.at[k]
        )
        for k in range(steps)
    ]
    for copy in copies:
        copy.start()
    start = start_ref[0]
    codes = pairs_ref[0:1, :] * LOC + pairs_ref[1:2, :]
    scale = potential_ref[...]
    tail_row = lax.broadcasted_iota(jnp.int32, (8, NB), 0)
    tail = jnp.where(tail_row == 1, start.astype(F32), 0.0)
    eye = upper(False) & ~upper(True)

    def send(row, col, block, last_rows):
        target = lax.rem(row, NDOM) * NCOL + lax.rem(col, NCOL)
        out_ref[target, 0:NB, :] = block.astype(BF16)
        out_ref[target, NB:ROWS, :] = last_rows.astype(BF16)

    for right in range(steps):
        copies[right].wait()
        right_rows = pl.ds(right * step_rows, step_rows)
        right_side = held[right_rows, :]
        weighted[right_rows, :] = (right_side.astype(F32) * scale).astype(BF16)
        for left in range(right + 1):
            tile = lax.dot_general(
                weighted[pl.ds(left * step_rows, step_rows), :],
                right_side,
                (((1,), (1,)), ((), ())),
                preferred_element_type=F32,
            )
            for a in (2 * left, 2 * left + 1):
                for b in (2 * right, 2 * right + 1):
                    block = tile[(a % 2) * NB : (a % 2 + 1) * NB, (b % 2) * NB : (b % 2 + 1) * NB]
                    gap = b - a
                    if gap < 0:
                        continue
                    if gap == 0 and a < LOC // 2:
                        diagonal[a] = block
                    elif gap == 0:
                        low = a - LOC // 2
                        packed = jnp.where(upper(False), diagonal[low], block)
                        extra = jnp.sum(jnp.where(eye, block, 0.0), axis=0, keepdims=True)
                        send(start + low, start + low, packed, jnp.where(tail_row == 0, extra, tail))
                    elif gap < LOC // 2:
                        send(start + a, start + b, block, tail)
                    elif gap == LOC // 2:
                        send(start + b, start + b, block, tail)
                    else:
                        listed = jnp.max(jnp.where(codes == a * LOC + b, 1.0, 0.0), axis=1, keepdims=True)
                        send(start + b, start + a, block * listed, tail)


def messages(domain_start, margin_pairs, potential, orbitals):
    rows = LOC * NB
    grid_points = orbitals.shape[-1]
    return pl.pallas_call(
        message_kernel,
        out_shape=jax.ShapeDtypeStruct((NDEV, ROWS, NB), BF16),
        in_specs=[SMEM, VMEM, VMEM, pl.BlockSpec(memory_space=pl.ANY)],
        out_specs=VMEM,
        scratch_shapes=[
            pltpu.VMEM((rows, grid_points), BF16),
            pltpu.VMEM((rows, grid_points), BF16),
            pltpu.VMEM((LOC // 2, NB, NB), F32),
            pltpu.SemaphoreType.DMA((LOC // 2,)),
        ],
        compiler_params=pltpu.CompilerParams(vmem_limit_bytes=40 << 20),
        cost_estimate=pl.CostEstimate(flops=5_000_000_000, bytes_accessed=9_000_000, transcendentals=0),
        name="blocks",
    )(domain_start, margin_pairs, potential, orbitals.reshape(rows, grid_points))


def wrap(value, size):
    return lax.rem(value + 2 * size, size)


def place():
    dom, col = lax.axis_index("dom"), lax.axis_index("col")
    return dom, col, wrap(col - dom, NDOM)


def sum_kernel(in_ref, direct_ref, turned_ref, total, extra_total):
    step = pl.program_id(0)
    _, col, kind = place()
    near = jnp.where(kind == 0, LOC // 2, kind)

    @pl.when(step == 0)
    def _():
        total[...] = jnp.zeros_like(total)
        extra_total[...] = jnp.zeros_like(extra_total)

    ends = in_ref[:, NB:ROWS, :].astype(F32)
    start = ends[:, 1, :].astype(jnp.int32)
    position = (col + NBLK - start) & (LOC - 1)
    half = ((start + position) & (NBLK - 1)) // LOC
    key = jnp.where(position >= near, 0, 2) + half
    chosen = [jnp.where(key == k, 1.0, 0.0) for k in range(4)]
    for k in (2, 3):
        extra_total[k - 2 : k - 1, :] += jnp.sum(ends[:, 0, :] * chosen[k], axis=0, keepdims=True)
    for tile in range(NB // 16):
        rows = pl.ds(tile * 16, 16)
        sums = [total[k, rows, :] for k in range(4)]
        for m in range(CHUNK):
            value = in_ref[m, rows, :].astype(F32)
            sums = [sums[k] + value * chosen[k][m : m + 1, :] for k in range(4)]
        for k in range(4):
            total[k, rows, :] = sums[k]

    @pl.when(step == NDEV // CHUNK - 1)
    def _():
        row = lax.broadcasted_iota(jnp.int32, (16, NB), 0)
        extra = jnp.where(row == 0, extra_total[0:1, :], jnp.where(row == 1, extra_total[1:2, :], 0.0)).astype(BF16)
        for k in range(4):
            plain = total[k]
            flipped = plain.T
            rows = pl.ds(k * NB, NB)
            direct_ref[rows, :] = (flipped if k < 2 else plain).astype(BF16)
            turned_ref[rows, :] = (plain if k < 2 else flipped).astype(BF16)
        direct_ref[4 * NB : HELD, :] = extra
        turned_ref[4 * NB : HELD, :] = extra


def sums(incoming):
    shape = jax.ShapeDtypeStruct((HELD, NB), BF16)
    return pl.pallas_call(
        sum_kernel,
        out_shape=(shape, shape),
        grid=(NDEV // CHUNK,),
        in_specs=[pl.BlockSpec((CHUNK, ROWS, NB), lambda i: (i, 0, 0))],
        out_specs=(pl.BlockSpec((HELD, NB), lambda i: (0, 0)),) * 2,
        scratch_shapes=[pltpu.VMEM((4, NB, NB), F32), pltpu.VMEM((2, NB), F32)],
        cost_estimate=pl.CostEstimate(flops=20_000_000, bytes_accessed=4_700_000, transcendentals=0),
        name="sums",
    )(incoming)


def diagonal_block(col, half, direct, turned):
    other = lax.rem(col + LOC * half + NBLK - NDOM, NBLK) // LOC
    first = direct[pl.ds((2 + half) * NB, NB), :].astype(F32)
    second = turned[pl.ds(pl.multiple_of((2 + other) * NB, NB), NB), :].astype(F32)
    ends = turned[4 * NB : HELD, :].astype(F32)
    extra = jnp.where(other == 0, ends[0:1, :], ends[1:2, :])
    above = jnp.where(upper(True), first + second, 0.0)
    eye = upper(False) & ~upper(True)
    return jnp.where(eye, first + extra, above + above.T)


def owned_blocks(dom, col, direct, turned, put):
    kind = wrap(col - dom, NDOM)
    near = jnp.where(kind == 0, LOC // 2, kind)
    other_near = NDOM - kind
    other_col = wrap(col - kind - NDOM, NCOL)
    for half in range(2):
        mine = col + LOC * half
        theirs = other_col + LOC * half
        put(wrap(mine - near, NBLK) // NDOM, half, direct[pl.ds(half * NB, NB), :])
        put(theirs // NDOM, wrap(theirs - other_near, NBLK) // LOC, turned[pl.ds(half * NB, NB), :])

    @pl.when(kind > 0)
    def _():
        for half in range(2):
            mine = col + LOC * half
            theirs = other_col + LOC * half
            rows = pl.ds((2 + half) * NB, NB)
            put(wrap(mine + LOC - kind, NBLK) // NDOM, half, direct[rows, :])
            put(theirs // NDOM, wrap(theirs + NDOM + kind, NBLK) // LOC, turned[rows, :])

    @pl.when(kind == 0)
    def _():
        for half in range(2):
            mine = col + LOC * half
            put(mine // NDOM, half, diagonal_block(col, half, direct, turned).astype(BF16))
            put(wrap(mine + LOC, NBLK) // NDOM, half, jnp.zeros((NB, NB), BF16))


def owned_kernel(direct_ref, turned_ref, out_ref):
    dom, col, _ = place()

    def put(row, half, block):
        out_ref[row, half] = block.astype(F32).T.astype(BF16)

    owned_blocks(dom, col, direct_ref, turned_ref, put)


def owned(direct, turned):
    return pl.pallas_call(
        owned_kernel,
        out_shape=jax.ShapeDtypeStruct((4, 2, NB, NB), BF16),
        in_specs=[VMEM, VMEM],
        out_specs=VMEM,
        cost_estimate=pl.CostEstimate(flops=1_000_000, bytes_accessed=550_000, transcendentals=0),
        name="owned",
    )(direct, turned)


def product_kernel(panel_ref, *refs):
    direct, turned = refs[0:4], refs[4:8]
    mine_ref, other_ref, left = refs[8:11]
    dom, col, _ = place()
    y, core = dom // 2, lax.rem(dom, 2)
    for k in range(4):
        their_y = wrap(y - k, 4)

        def put(row, half, block, their_y=their_y):
            place_of = pl.multiple_of((their_y * 4 + row) * NB, NB)
            left[pl.ds(half * NB, NB) if isinstance(half, int) else pl.ds(pl.multiple_of(half * NB, NB), NB),
                 pl.ds(place_of, NB)] = block

        owned_blocks(2 * their_y + core, col, direct[k], turned[k], put)
    depth = 4 * NB
    for j in range(4):
        part = jnp.zeros((2 * NB, NB), F32)
        for their_y in range(4):
            part = part + jnp.dot(
                left[:, their_y * depth : (their_y + 1) * depth],
                panel_ref[their_y * 4 + j],
                preferred_element_type=F32,
            )
        part = part.reshape(2, NB, NB)

        @pl.when(core == j // 2)
        def _():
            mine_ref[:, j % 2] = part

        @pl.when(core != j // 2)
        def _():
            other_ref[:, j % 2] = part


def product_parts(panel, direct, turned):
    shape = jax.ShapeDtypeStruct((2, 2, NB, NB), F32)
    return pl.pallas_call(
        product_kernel,
        out_shape=(shape, shape),
        in_specs=[VMEM] * 9,
        out_specs=(VMEM, VMEM),
        scratch_shapes=[pltpu.VMEM((2 * NB, 16 * NB), BF16)],
        compiler_params=pltpu.CompilerParams(vmem_limit_bytes=32 << 20),
        cost_estimate=pl.CostEstimate(flops=540_000_000, bytes_accessed=4_000_000, transcendentals=0),
        name="product",
    )(panel, *direct, *turned)


def device(y, core, col):
    return (2 * y + core) * NCOL + col


def partner(dom, col):
    kind = (col - dom) % NDOM
    return (col % NDOM) * NCOL + (col - kind - NDOM) % NCOL


PLACES = [(y, core, col) for y in range(4) for core in range(2) for col in range(NCOL)]


def around(step):
    return [(device(y, core, col), device((y + step) % 4, core, col)) for y, core, col in PLACES]


def from_partner(step):
    return [(partner(2 * y + core, col), device((y + step) % 4, core, col)) for y, core, col in PLACES]


def shards(orbitals, potential, domain_start, margin_pairs, coefficients):
    to_row = [(device(y, core, s), device(s // 4, core, 4 * y + s % 4)) for y, core, s in PLACES]
    rows = lax.ppermute(coefficients.reshape(4 * NB, NB), AXES, to_row)
    panel = lax.all_gather(rows, "col", axis=0, tiled=False)
    outgoing = messages(domain_start, margin_pairs[0], potential, orbitals)
    incoming = lax.all_to_all(outgoing, AXES, split_axis=0, concat_axis=0, tiled=True)
    direct, turned = sums(incoming)
    near = [direct] + [lax.ppermute(direct, AXES, around(k)) for k in (1, 2, 3)]
    far = [lax.ppermute(turned, AXES, from_partner(k)) for k in range(4)]
    potential_blocks = owned(direct, far[0]).reshape(4, 1, 2, 1, NB, NB)
    mine, other = product_parts(panel, near, far)
    swap = [(device(y, core, col), device(y, 1 - core, col)) for y, core, col in PLACES]
    product = mine + lax.ppermute(other, AXES, swap)
    return potential_blocks, jnp.swapaxes(product, 1, 2).reshape(2, 1, NB, 2, NB)


def solution(mesh):
    placed = (
        P(AXES, None, None, None),
        P(AXES, None),
        P(AXES),
        P(AXES, None, None),
        P(None, "dom", None, "col", None),
    )
    return jax.shard_map(
        shards,
        mesh=mesh,
        in_specs=placed,
        out_specs=(P(None, "dom", None, "col", None, None), P(None, "col", None, "dom", None)),
        check_vma=False,
    )
```

```python
import functools

import jax
import jax.numpy as jnp
from jax import lax
from jax.experimental import pallas as pl
from jax.experimental.pallas import tpu as pltpu
from jax.sharding import PartitionSpec as P

F32 = jnp.float32
BF16 = jnp.bfloat16
AXES = ("dom", "col")
NB = 128
LOC = 16
NBLK = 32
NDOM = 8
NCOL = 16
NDEV = NDOM * NCOL
HELD = 4 * NB
ROWS = NB + 8
CHUNK = 64
TILE = 16
VMEM = pl.BlockSpec(memory_space=pltpu.VMEM)
HBM = pl.BlockSpec(memory_space=pltpu.HBM)
SMEM = pl.BlockSpec(memory_space=pltpu.SMEM)


def upper(strict):
    row = lax.broadcasted_iota(jnp.int32, (NB, NB), 0)
    col = lax.broadcasted_iota(jnp.int32, (NB, NB), 1)
    return row < col if strict else row <= col


def home(kind, col):
    return kind ^ (col & 1)


def message_kernel(
    start_ref, pairs_ref, potential_ref, orbitals_ref, out_ref, held, weighted, diagonal, pairs, potential, sems
):
    step_rows = 2 * NB
    steps = LOC // 2
    small = [
        pltpu.make_async_copy(pairs_ref, pairs, sems.at[steps]),
        pltpu.make_async_copy(potential_ref, potential, sems.at[steps + 1]),
    ]
    copies = [
        pltpu.make_async_copy(
            orbitals_ref.at[pl.ds(k * step_rows, step_rows)], held.at[pl.ds(k * step_rows, step_rows)], sems.at[k]
        )
        for k in range(steps)
    ]
    for copy in small + copies:
        copy.start()
    start = start_ref[0]
    tail_row = lax.broadcasted_iota(jnp.int32, (8, NB), 0)
    tail = jnp.where(tail_row == 1, start.astype(F32), 0.0)
    eye = upper(False) & ~upper(True)
    for copy in small:
        copy.wait()
    codes = pairs[0:1, :] * LOC + pairs[1:2, :]
    scale = potential[...]

    def send(kind, col, block, last_rows):
        col = lax.rem(col, NCOL)
        target = home(kind, col) * NCOL + col
        if block is not None:
            out_ref[target, 0:NB, :] = block.astype(BF16)
        if last_rows is not None:
            out_ref[target, NB:ROWS, :] = last_rows.astype(BF16)

    for right in range(steps):
        copies[right].wait()
        right_rows = pl.ds(right * step_rows, step_rows)
        right_side = held[right_rows, :]
        weighted[right_rows, :] = (right_side.astype(F32) * scale).astype(BF16)
        for left in range(right + 1):
            tile = lax.dot_general(
                weighted[pl.ds(left * step_rows, step_rows), :],
                right_side,
                (((1,), (1,)), ((), ())),
                preferred_element_type=F32,
            )
            for a in (2 * left, 2 * left + 1):
                for b in (2 * right, 2 * right + 1):
                    block = tile[(a % 2) * NB : (a % 2 + 1) * NB, (b % 2) * NB : (b % 2 + 1) * NB]
                    gap = b - a
                    if gap < 0:
                        continue
                    if gap == 0 and a < LOC // 2:
                        diagonal[a] = block
                    elif gap == 0:
                        low = a - LOC // 2
                        send(0, start + low, jnp.where(upper(False), diagonal[low], block), tail)
                        extra = jnp.sum(jnp.where(eye, block, 0.0), axis=0, keepdims=True)
                        send(0, start + a, None, jnp.where(tail_row == 0, extra, tail))
                    elif gap < LOC // 2:
                        send(gap, start + b, block, tail)
                    elif gap == LOC // 2:
                        send(0, start + b, block, None)
                    else:
                        listed = jnp.max(jnp.where(codes == a * LOC + b, 1.0, 0.0), axis=1, keepdims=True)
                        send(LOC - gap, start + a, block * listed, tail)


def in_hbm(value):
    return pltpu.with_memory_space_constraint(value, pltpu.HBM)


def messages(domain_start, margin_pairs, potential, orbitals):
    rows = LOC * NB
    grid_points = orbitals.shape[-1]
    return pl.pallas_call(
        message_kernel,
        out_shape=pltpu.HBM((NDEV, ROWS, NB), BF16),
        in_specs=[SMEM, HBM, HBM, HBM],
        out_specs=VMEM,
        scratch_shapes=[
            pltpu.VMEM((rows, grid_points), BF16),
            pltpu.VMEM((rows, grid_points), BF16),
            pltpu.VMEM((LOC // 2, NB, NB), F32),
            pltpu.VMEM(margin_pairs.shape, jnp.int32),
            pltpu.VMEM(potential.shape, F32),
            pltpu.SemaphoreType.DMA((LOC // 2 + 2,)),
        ],
        compiler_params=pltpu.CompilerParams(vmem_limit_bytes=40 << 20),
        cost_estimate=pl.CostEstimate(flops=5_000_000_000, bytes_accessed=9_000_000, transcendentals=0),
        name="blocks",
    )(domain_start, in_hbm(margin_pairs), in_hbm(potential), in_hbm(orbitals.reshape(rows, grid_points)))


def wrap(value, size):
    return lax.rem(value + 2 * size, size)


def place():
    dom, col = lax.axis_index("dom"), lax.axis_index("col")
    return dom, col, home(dom, col)


def sum_kernel(in_ref, direct_ref, turned_ref, total, extra_total):
    step = pl.program_id(0)
    _, col, kind = place()
    near = jnp.where(kind == 0, LOC // 2, kind)

    @pl.when(step == 0)
    def _():
        total[...] = jnp.zeros_like(total)
        extra_total[...] = jnp.zeros_like(extra_total)

    ends = in_ref[:, NB:ROWS, :].astype(F32)
    start = ends[:, 1, :].astype(jnp.int32)
    position = (col + NBLK - start) & (LOC - 1)
    half = ((start + position) & (NBLK - 1)) // LOC
    key = jnp.where(position >= near, 0, 2) + half
    for k in range(2):
        extra_total[k : k + 1, :] += jnp.sum(jnp.where(key == k, ends[:, 0, :], 0.0), axis=0, keepdims=True)
    depth = CHUNK * TILE
    sublane = lax.broadcasted_iota(jnp.int32, (CHUNK, depth), 0)
    lane = lax.broadcasted_iota(jnp.int32, (CHUNK, depth), 1)
    keys = jnp.concatenate([key] * (depth // NB), axis=1)
    lane_key = jnp.sum(jnp.where(sublane == lane // TILE, keys, 0), axis=0, keepdims=True)
    row = lax.broadcasted_iota(jnp.int32, (4 * TILE, depth), 0)
    lane = lax.broadcasted_iota(jnp.int32, (4 * TILE, depth), 1)
    chosen = jnp.where((row // TILE == lane_key) & ((row & (TILE - 1)) == (lane & (TILE - 1))), 1.0, 0.0).astype(BF16)
    for pair in range(NB // TILE // 2):
        first = pair * 2 * TILE
        sides = [in_ref[:, first + t * TILE : first + (t + 1) * TILE, :].reshape(depth, NB) for t in range(2)]
        total[:, pair * 2 * NB : (pair + 1) * 2 * NB] += jnp.dot(
            chosen, jnp.concatenate(sides, axis=1), preferred_element_type=F32
        )

    @pl.when(step == NDEV // CHUNK - 1)
    def _():
        eye = upper(False) & ~upper(True)
        for k in range(4):
            plain = jnp.concatenate(
                [total[k * TILE : (k + 1) * TILE, t * NB : (t + 1) * NB] for t in range(NB // TILE)], axis=0
            )
            if k >= 2:
                plain = plain + jnp.where(eye, extra_total[k - 2 : k - 1, :], 0.0)
            flipped = plain.T
            rows = pl.ds(k * NB, NB)
            direct_ref[rows, :] = (flipped if k < 2 else plain).astype(BF16)
            turned_ref[rows, :] = (plain if k < 2 else flipped).astype(BF16)


def sums(incoming):
    shape = jax.ShapeDtypeStruct((HELD, NB), BF16)
    return pl.pallas_call(
        sum_kernel,
        out_shape=(shape, shape),
        grid=(NDEV // CHUNK,),
        in_specs=[pl.BlockSpec((CHUNK, ROWS, NB), lambda i: (i, 0, 0))],
        out_specs=(pl.BlockSpec((HELD, NB), lambda i: (0, 0)),) * 2,
        scratch_shapes=[pltpu.VMEM((4 * TILE, NB // TILE * NB), F32), pltpu.VMEM((2, NB), F32)],
        cost_estimate=pl.CostEstimate(flops=300_000_000, bytes_accessed=4_700_000, transcendentals=0),
        name="sums",
    )(incoming)


def diagonal_block(col, half, direct, turned):
    other = lax.rem(col + LOC * half + NBLK - NDOM, NBLK) // LOC
    first = direct[pl.ds((2 + half) * NB, NB), :].astype(F32)
    second = turned[pl.ds(pl.multiple_of((2 + other) * NB, NB), NB), :].astype(F32)
    above = jnp.where(upper(True), first + second, 0.0)
    eye = upper(False) & ~upper(True)
    return jnp.where(eye, first, above + above.T)


def column_blocks(kind, col, direct, turned, put):
    near = jnp.where(kind == 0, LOC // 2, kind)
    other_col = lax.rem(col + near, NCOL)
    for half in range(2):
        mine = col + LOC * half
        theirs = other_col + LOC * half
        put(wrap(mine - near, NBLK), half, direct[pl.ds(half * NB, NB), :])
        put(theirs, wrap(theirs - near, NBLK) // LOC, turned[pl.ds(half * NB, NB), :])

    @pl.when(kind > 0)
    def _():
        for half in range(2):
            mine = col + LOC * half
            theirs = other_col + LOC * half
            rows = pl.ds((2 + half) * NB, NB)
            put(wrap(mine + LOC - kind, NBLK), half, direct[rows, :])
            put(theirs, wrap(theirs + LOC - kind, NBLK) // LOC, turned[rows, :])

    @pl.when(kind == 0)
    def _():
        for half in range(2):
            mine = col + LOC * half
            put(mine, half, diagonal_block(col, half, direct, turned).astype(BF16))
            put(wrap(mine + LOC, NBLK), half, jnp.zeros((NB, NB), BF16))


def owned_kernel(in_ref, out_ref):
    for row in range(4):
        for half in range(2):
            block = in_ref[half * NB : (half + 1) * NB, row * NB : (row + 1) * NB]
            out_ref[row, half] = block.astype(F32).T.astype(BF16)


def owned(slab):
    return pl.pallas_call(
        owned_kernel,
        out_shape=jax.ShapeDtypeStruct((4, 2, NB, NB), BF16),
        in_specs=[VMEM],
        out_specs=VMEM,
        cost_estimate=pl.CostEstimate(flops=1_000_000, bytes_accessed=550_000, transcendentals=0),
        name="owned",
    )(slab)


def ring_place(place_on_ring, core, k):
    even = jnp.where(lax.rem(place_on_ring, 2) == 0, place_on_ring + 1, place_on_ring - 1)
    odd = 3 - place_on_ring
    first, second = jnp.where(core == 0, even, odd), jnp.where(core == 0, odd, even)
    return (place_on_ring, first, second, wrap(place_on_ring + 2, 4))[k]


def product_kernel(*refs):
    upper_panel, lower_panel, direct, turned = refs[0:2], refs[2:4], refs[4:6], refs[6:8]
    mine_ref, other_ref, slab_ref, left = refs[8:12]
    dom, col, _ = place()
    y, core = dom // 2, lax.rem(dom, 2)
    depth = 2 * NB

    def put(block_row, half, block):
        slot = (lax.rem(block_row, NDOM) // 2) * 4 + block_row // NDOM
        rows = pl.ds(half * NB if isinstance(half, int) else pl.multiple_of(half * NB, NB), NB)
        left[rows, pl.ds(pl.multiple_of(slot * NB, NB), NB)] = block

    for k in range(4):
        kind = home(2 * ring_place(y, core, k) + core, col)
        column_blocks(kind, col, direct[k // 2].at[k % 2], turned[k // 2].at[k % 2], put)
    slab_ref[...] = left[:, pl.ds(pl.multiple_of(y * (2 * depth), depth), 2 * depth)]
    z, x = col // 4, lax.rem(col, 4)
    for x_step in range(4):
        part = jnp.zeros((2 * NB, NB), F32)
        for z_step in range(4):
            start = pl.multiple_of(ring_place(z, core, z_step) * (2 * depth), depth)
            part = part + jnp.dot(
                left[:, pl.ds(start, depth)],
                upper_panel[x_step // 2][x_step % 2, z_step],
                preferred_element_type=F32,
            )
            part = part + jnp.dot(
                left[:, pl.ds(pl.multiple_of(start + depth, depth), depth)],
                lower_panel[z_step // 2][z_step % 2, x_step],
                preferred_element_type=F32,
            )
        part = part.reshape(2, NB, NB)
        j = ring_place(x, core, x_step)

        @pl.when(core == j // 2)
        def _():
            mine_ref[:, lax.rem(j, 2)] = part

        @pl.when(core != j // 2)
        def _():
            other_ref[:, lax.rem(j, 2)] = part


def product_parts(panels, direct, turned):
    shape = jax.ShapeDtypeStruct((2, 2, NB, NB), F32)
    return pl.pallas_call(
        product_kernel,
        out_shape=(shape, shape, jax.ShapeDtypeStruct((2 * NB, 4 * NB), BF16)),
        in_specs=[VMEM] * 8,
        out_specs=(VMEM, VMEM, VMEM),
        scratch_shapes=[pltpu.VMEM((2 * NB, 16 * NB), BF16)],
        compiler_params=pltpu.CompilerParams(vmem_limit_bytes=32 << 20),
        cost_estimate=pl.CostEstimate(flops=540_000_000, bytes_accessed=4_000_000, transcendentals=0),
        name="product",
    )(*panels, *direct, *turned)


def device(y, core, col):
    return (2 * y + core) * NCOL + col


PLACES = [(y, core, col) for y in range(4) for core in range(2) for col in range(NCOL)]
TO_ROW = [(device(y, core, col), device(col // 4, core, 4 * y + col % 4)) for y, core, col in PLACES]
TO_OTHER_CORE = [(device(y, core, col), device(y, 1 - core, col)) for y, core, col in PLACES]


def from_partner():
    pairs = []
    for kind in range(NDOM):
        for col in range(NCOL):
            source = (col + (kind or LOC // 2)) % NCOL
            pairs.append((home(kind, source) * NCOL + source, home(kind, col) * NCOL + col))
    return pairs


def exchange(axis, step):
    pairs = []
    for y, core, col in PLACES:
        at = dict(y=y, z=col // 4, x=col % 4)
        at[axis] = at[axis] ^ 1 if core == step else 3 - at[axis]
        pairs.append((device(y, core, col), device(at["y"], core, 4 * at["z"] + at["x"])))
    return pairs


def first_near(value, axis):
    return jnp.stack([value, lax.ppermute(value, AXES, exchange(axis, 0))])


def second_near(pair, axis):
    return lax.ppermute(pair, AXES, exchange(axis, 1))


def shards(orbitals, potential, domain_start, margin_pairs, coefficients):
    own = lax.ppermute(coefficients.reshape(4 * NB, NB), AXES, TO_ROW)
    outgoing = messages(domain_start, margin_pairs[0], potential, orbitals)
    outgoing, own = lax.optimization_barrier((outgoing, own))
    incoming = lax.all_to_all(outgoing, AXES, split_axis=0, concat_axis=0, tiled=True)
    above, below = first_near(own[: 2 * NB], "z"), first_near(own[2 * NB :], "x")
    incoming, above, below = lax.optimization_barrier((incoming, above, below))
    above = jnp.concatenate([above, second_near(above, "z")])
    below = jnp.concatenate([below, second_near(below, "x")])
    direct, turned = sums(incoming)
    direct, turned, above, below = lax.optimization_barrier((direct, turned, above, below))
    turned = lax.ppermute(turned, AXES, from_partner())
    direct = first_near(direct, "y")
    above, below = first_near(above, "x"), first_near(below, "z")
    turned, direct, above, below = lax.optimization_barrier((turned, direct, above, below))
    turned = first_near(turned, "y")
    direct = direct, second_near(direct, "y")
    panels = above, second_near(above, "x"), below, second_near(below, "z")
    turned = turned, second_near(turned, "y")
    mine, other, slab = product_parts(panels, direct, turned)
    product = mine + lax.ppermute(other, AXES, TO_OTHER_CORE)
    potential_blocks = owned(slab).reshape(4, 1, 2, 1, NB, NB)
    return potential_blocks, jnp.swapaxes(product, 1, 2).reshape(2, 1, NB, 2, NB)


def solution(mesh):
    placed = (
        P(AXES, None, None, None),
        P(AXES, None),
        P(AXES),
        P(AXES, None, None),
        P(None, "dom", None, "col", None),
    )
    return jax.shard_map(
        shards,
        mesh=mesh,
        in_specs=placed,
        out_specs=(P(None, "dom", None, "col", None, None), P(None, "col", None, "dom", None)),
        check_vma=False,
    )
```

```python
import functools

import jax
import jax.numpy as jnp
from jax import lax
from jax.experimental import pallas as pl
from jax.experimental.pallas import tpu as pltpu
from jax.sharding import PartitionSpec as P

F32 = jnp.float32
BF16 = jnp.bfloat16
AXES = ("dom", "col")
NB = 128
LOC = 16
NBLK = 32
NDOM = 8
NCOL = 16
NDEV = NDOM * NCOL
HELD = 4 * NB
SUB = 8
TILES = NB // SUB
ROWS = NB + SUB
CHUNK = 64
TILE = 16
VMEM = pl.BlockSpec(memory_space=pltpu.VMEM)
HBM = pl.BlockSpec(memory_space=pltpu.HBM)
SMEM = pl.BlockSpec(memory_space=pltpu.SMEM)


def upper(strict):
    row = lax.broadcasted_iota(jnp.int32, (NB, NB), 0)
    col = lax.broadcasted_iota(jnp.int32, (NB, NB), 1)
    return row < col if strict else row <= col


def home(kind, col):
    return kind ^ (col & 1)


def message_kernel(
    start_ref, pairs_ref, potential_ref, orbitals_ref, out_ref,
    held, weighted, diagonal, outgoing, pairs, potential, sems, out_sem,
):
    step_rows = 2 * NB
    steps = LOC // 2
    small = [
        pltpu.make_async_copy(pairs_ref, pairs, sems.at[steps]),
        pltpu.make_async_copy(potential_ref, potential, sems.at[steps + 1]),
    ]
    copies = [
        pltpu.make_async_copy(
            orbitals_ref.at[pl.ds(k * step_rows, step_rows)], held.at[pl.ds(k * step_rows, step_rows)], sems.at[k]
        )
        for k in range(steps)
    ]
    for copy in small + copies:
        copy.start()
    start = start_ref[0]
    tail_row = lax.broadcasted_iota(jnp.int32, (8, NB), 0)
    tail = jnp.where(tail_row == 1, start.astype(F32), 0.0)
    eye = upper(False) & ~upper(True)
    for copy in small:
        copy.wait()
    codes = pairs[0:1, :] * LOC + pairs[1:2, :]
    scale = potential[...]

    slots = {}

    def send(kind, col, block, last_rows):
        slot = slots.setdefault((kind, col), len(slots))
        if block is not None:
            outgoing[slot, 0:TILES] = block.reshape(TILES, SUB, NB).astype(BF16)
        if last_rows is None:
            return
        outgoing[slot, TILES] = last_rows.astype(BF16)
        column = lax.rem(start + col, NCOL)
        target = home(kind, column) * NCOL + column
        pltpu.make_async_copy(outgoing.at[slot], out_ref.at[target], out_sem).start()

    for right in range(steps):
        copies[right].wait()
        right_rows = pl.ds(right * step_rows, step_rows)
        right_side = held[right_rows, :]
        weighted[right_rows, :] = (right_side.astype(F32) * scale).astype(BF16)
        for left in range(right + 1):
            tile = lax.dot_general(
                weighted[pl.ds(left * step_rows, step_rows), :],
                right_side,
                (((1,), (1,)), ((), ())),
                preferred_element_type=F32,
            )
            for a in (2 * left, 2 * left + 1):
                for b in (2 * right, 2 * right + 1):
                    block = tile[(a % 2) * NB : (a % 2 + 1) * NB, (b % 2) * NB : (b % 2 + 1) * NB]
                    gap = b - a
                    if gap < 0:
                        continue
                    if gap == 0 and a < LOC // 2:
                        diagonal[a] = block
                    elif gap == 0:
                        low = a - LOC // 2
                        send(0, low, jnp.where(upper(False), diagonal[low], block), tail)
                        extra = jnp.sum(jnp.where(eye, block, 0.0), axis=0, keepdims=True)
                        send(0, a, None, jnp.where(tail_row == 0, extra, tail))
                    elif gap < LOC // 2:
                        send(gap, b, block, tail)
                    elif gap == LOC // 2:
                        send(0, b, block, None)
                    else:
                        listed = jnp.max(jnp.where(codes == a * LOC + b, 1.0, 0.0), axis=1, keepdims=True)
                        send(LOC - gap, a, block * listed, tail)
    pltpu.make_async_copy(outgoing, out_ref, out_sem).wait()


def in_hbm(value):
    return pltpu.with_memory_space_constraint(value, pltpu.HBM)


def messages(domain_start, margin_pairs, potential, orbitals):
    rows = LOC * NB
    grid_points = orbitals.shape[-1]
    return pl.pallas_call(
        message_kernel,
        out_shape=pltpu.HBM((NDEV, TILES + 1, SUB, NB), BF16),
        in_specs=[SMEM, HBM, HBM, HBM],
        out_specs=HBM,
        scratch_shapes=[
            pltpu.VMEM((rows, grid_points), BF16),
            pltpu.VMEM((rows, grid_points), BF16),
            pltpu.VMEM((LOC // 2, NB, NB), F32),
            pltpu.VMEM((NDEV, TILES + 1, SUB, NB), BF16),
            pltpu.VMEM(margin_pairs.shape, jnp.int32),
            pltpu.VMEM(potential.shape, F32),
            pltpu.SemaphoreType.DMA((LOC // 2 + 2,)),
            pltpu.SemaphoreType.DMA,
        ],
        compiler_params=pltpu.CompilerParams(vmem_limit_bytes=40 << 20),
        cost_estimate=pl.CostEstimate(flops=5_000_000_000, bytes_accessed=9_000_000, transcendentals=0),
        name="blocks",
    )(domain_start, in_hbm(margin_pairs), in_hbm(potential), in_hbm(orbitals.reshape(rows, grid_points))).reshape(NDEV, ROWS, NB)


def wrap(value, size):
    return lax.rem(value + 2 * size, size)


def place():
    dom, col = lax.axis_index("dom"), lax.axis_index("col")
    return dom, col, home(dom, col)


def sum_kernel(in_ref, direct_ref, turned_ref, total, extra_total):
    step = pl.program_id(0)
    _, col, kind = place()
    near = jnp.where(kind == 0, LOC // 2, kind)

    @pl.when(step == 0)
    def _():
        total[...] = jnp.zeros_like(total)
        extra_total[...] = jnp.zeros_like(extra_total)

    ends = in_ref[:, NB:ROWS, :].astype(F32)
    start = ends[:, 1, :].astype(jnp.int32)
    position = (col + NBLK - start) & (LOC - 1)
    half = ((start + position) & (NBLK - 1)) // LOC
    key = jnp.where(position >= near, 0, 2) + half
    for k in range(2):
        extra_total[k : k + 1, :] += jnp.sum(jnp.where(key == k, ends[:, 0, :], 0.0), axis=0, keepdims=True)
    depth = CHUNK * TILE
    sublane = lax.broadcasted_iota(jnp.int32, (CHUNK, depth), 0)
    lane = lax.broadcasted_iota(jnp.int32, (CHUNK, depth), 1)
    keys = jnp.concatenate([key] * (depth // NB), axis=1)
    lane_key = jnp.sum(jnp.where(sublane == lane // TILE, keys, 0), axis=0, keepdims=True)
    row = lax.broadcasted_iota(jnp.int32, (4 * TILE, depth), 0)
    lane = lax.broadcasted_iota(jnp.int32, (4 * TILE, depth), 1)
    chosen = jnp.where((row // TILE == lane_key) & ((row & (TILE - 1)) == (lane & (TILE - 1))), 1.0, 0.0).astype(BF16)
    for pair in range(NB // TILE // 2):
        first = pair * 2 * TILE
        sides = [in_ref[:, first + t * TILE : first + (t + 1) * TILE, :].reshape(depth, NB) for t in range(2)]
        total[:, pair * 2 * NB : (pair + 1) * 2 * NB] += jnp.dot(
            chosen, jnp.concatenate(sides, axis=1), preferred_element_type=F32
        )

    @pl.when(step == NDEV // CHUNK - 1)
    def _():
        eye = upper(False) & ~upper(True)
        for k in range(4):
            plain = jnp.concatenate(
                [total[k * TILE : (k + 1) * TILE, t * NB : (t + 1) * NB] for t in range(NB // TILE)], axis=0
            )
            if k >= 2:
                plain = plain + jnp.where(eye, extra_total[k - 2 : k - 1, :], 0.0)
            flipped = plain.T
            rows = pl.ds(k * NB, NB)
            direct_ref[rows, :] = (flipped if k < 2 else plain).astype(BF16)
            turned_ref[rows, :] = (plain if k < 2 else flipped).astype(BF16)


def sums(incoming):
    shape = jax.ShapeDtypeStruct((HELD, NB), BF16)
    return pl.pallas_call(
        sum_kernel,
        out_shape=(shape, shape),
        grid=(NDEV // CHUNK,),
        in_specs=[pl.BlockSpec((CHUNK, ROWS, NB), lambda i: (i, 0, 0))],
        out_specs=(pl.BlockSpec((HELD, NB), lambda i: (0, 0)),) * 2,
        scratch_shapes=[pltpu.VMEM((4 * TILE, NB // TILE * NB), F32), pltpu.VMEM((2, NB), F32)],
        cost_estimate=pl.CostEstimate(flops=300_000_000, bytes_accessed=4_700_000, transcendentals=0),
        name="sums",
    )(incoming)


def diagonal_block(col, half, direct, turned):
    other = lax.rem(col + LOC * half + NBLK - NDOM, NBLK) // LOC
    first = direct[pl.ds((2 + half) * NB, NB), :].astype(F32)
    second = turned[pl.ds(pl.multiple_of((2 + other) * NB, NB), NB), :].astype(F32)
    above = jnp.where(upper(True), first + second, 0.0)
    eye = upper(False) & ~upper(True)
    return jnp.where(eye, first, above + above.T)


def column_blocks(kind, col, direct, turned, put):
    near = jnp.where(kind == 0, LOC // 2, kind)
    other_col = lax.rem(col + near, NCOL)
    for half in range(2):
        mine = col + LOC * half
        theirs = other_col + LOC * half
        put(wrap(mine - near, NBLK), half, direct[pl.ds(half * NB, NB), :])
        put(theirs, wrap(theirs - near, NBLK) // LOC, turned[pl.ds(half * NB, NB), :])

    @pl.when(kind > 0)
    def _():
        for half in range(2):
            mine = col + LOC * half
            theirs = other_col + LOC * half
            rows = pl.ds((2 + half) * NB, NB)
            put(wrap(mine + LOC - kind, NBLK), half, direct[rows, :])
            put(theirs, wrap(theirs + LOC - kind, NBLK) // LOC, turned[rows, :])

    @pl.when(kind == 0)
    def _():
        for half in range(2):
            mine = col + LOC * half
            put(mine, half, diagonal_block(col, half, direct, turned).astype(BF16))
            put(wrap(mine + LOC, NBLK), half, jnp.zeros((NB, NB), BF16))


def ring_place(place_on_ring, core, k):
    even = jnp.where(lax.rem(place_on_ring, 2) == 0, place_on_ring + 1, place_on_ring - 1)
    odd = 3 - place_on_ring
    first, second = jnp.where(core == 0, even, odd), jnp.where(core == 0, odd, even)
    return (place_on_ring, first, second, wrap(place_on_ring + 2, 4))[k]


def half_product(panels, left, core, z, x, wanted, out_ref):
    upper_panel, lower_panel = panels[0:2], panels[2:4]
    depth = 2 * NB

    def add_up(steps):
        part = jnp.zeros((2 * NB, 2 * NB), F32)
        for z_step in range(4):
            start = pl.multiple_of(ring_place(z, core, z_step) * (2 * depth), depth)
            above = [upper_panel[k // 2][k % 2, z_step] for k in steps]
            below = [lower_panel[z_step // 2][z_step % 2, k] for k in steps]
            part = part + jnp.dot(
                left[:, pl.ds(start, depth)], jnp.concatenate(above, axis=1), preferred_element_type=F32
            )
            part = part + jnp.dot(
                left[:, pl.ds(pl.multiple_of(start + depth, depth), depth)],
                jnp.concatenate(below, axis=1),
                preferred_element_type=F32,
            )
        for i, k in enumerate(steps):
            place_of = lax.rem(ring_place(x, core, k), 2)
            out_ref[:, place_of] = part[:, i * NB : (i + 1) * NB].reshape(2, NB, NB)

    near = wanted == x // 2
    for on, steps in (
        (near & (core == 0), (0, 1)),
        (~near & (core == 0), (2, 3)),
        (near & (core == 1), (0, 2)),
        (~near & (core == 1), (1, 3)),
    ):
        pl.when(on)(functools.partial(add_up, steps))


def other_kernel(*refs):
    panels, direct, turned = refs[0:4], refs[4:6], refs[6:8]
    other_ref, left = refs[8:10]
    dom, col, _ = place()
    y, core = dom // 2, lax.rem(dom, 2)

    def put(block_row, half, block):
        slot = (lax.rem(block_row, NDOM) // 2) * 4 + block_row // NDOM
        rows = pl.ds(half * NB if isinstance(half, int) else pl.multiple_of(half * NB, NB), NB)
        left[rows, pl.ds(pl.multiple_of(slot * NB, NB), NB)] = block

    for k in range(4):
        kind = home(2 * ring_place(y, core, k) + core, col)
        column_blocks(kind, col, direct[k // 2].at[k % 2], turned[k // 2].at[k % 2], put)
    half_product(panels, left, core, col // 4, lax.rem(col, 4), 1 - core, other_ref)


def mine_kernel(*refs):
    panels, left, mine_ref, blocks_ref = refs[0:4], refs[4], refs[5], refs[6]
    dom, col, _ = place()
    y, core = dom // 2, lax.rem(dom, 2)
    half_product(panels, left, core, col // 4, lax.rem(col, 4), core, mine_ref)
    for row in range(4):
        column = pl.ds(pl.multiple_of((y * 4 + row) * NB, NB), NB)
        for half in range(2):
            block = left[half * NB : (half + 1) * NB, column]
            blocks_ref[row, half] = block.astype(F32).T.astype(BF16)


def product_for_other(panels, direct, turned):
    return pl.pallas_call(
        other_kernel,
        out_shape=(jax.ShapeDtypeStruct((2, 2, NB, NB), F32), jax.ShapeDtypeStruct((2 * NB, 16 * NB), BF16)),
        in_specs=[VMEM] * 8,
        out_specs=(VMEM, VMEM),
        compiler_params=pltpu.CompilerParams(vmem_limit_bytes=32 << 20),
        cost_estimate=pl.CostEstimate(flops=270_000_000, bytes_accessed=4_000_000, transcendentals=0),
        name="other",
    )(*panels, *direct, *turned)


def product_for_me(panels, left):
    return pl.pallas_call(
        mine_kernel,
        out_shape=(jax.ShapeDtypeStruct((2, 2, NB, NB), F32), jax.ShapeDtypeStruct((4, 2, NB, NB), BF16)),
        in_specs=[VMEM] * 5,
        out_specs=(VMEM, VMEM),
        compiler_params=pltpu.CompilerParams(vmem_limit_bytes=32 << 20),
        cost_estimate=pl.CostEstimate(flops=270_000_000, bytes_accessed=4_000_000, transcendentals=0),
        name="mine",
    )(*panels, left)


def device(y, core, col):
    return (2 * y + core) * NCOL + col


PLACES = [(y, core, col) for y in range(4) for core in range(2) for col in range(NCOL)]
TO_ROW = [(device(y, core, col), device(col // 4, core, 4 * y + col % 4)) for y, core, col in PLACES]
TO_OTHER_CORE = [(device(y, core, col), device(y, 1 - core, col)) for y, core, col in PLACES]


def from_partner():
    pairs = []
    for kind in range(NDOM):
        for col in range(NCOL):
            source = (col + (kind or LOC // 2)) % NCOL
            pairs.append((home(kind, source) * NCOL + source, home(kind, col) * NCOL + col))
    return pairs


def exchange(axis, step):
    pairs = []
    for y, core, col in PLACES:
        at = dict(y=y, z=col // 4, x=col % 4)
        at[axis] = at[axis] ^ 1 if core == step else 3 - at[axis]
        pairs.append((device(y, core, col), device(at["y"], core, 4 * at["z"] + at["x"])))
    return pairs


def first_near(value, axis):
    return jnp.stack([value, lax.ppermute(value, AXES, exchange(axis, 0))])


def second_near(pair, axis):
    return lax.ppermute(pair, AXES, exchange(axis, 1))


def shards(orbitals, potential, domain_start, margin_pairs, coefficients):
    own = lax.ppermute(coefficients.reshape(4 * NB, NB), AXES, TO_ROW)
    outgoing = messages(domain_start, margin_pairs[0], potential, orbitals)
    outgoing, own = lax.optimization_barrier((outgoing, own))
    incoming = lax.all_to_all(outgoing, AXES, split_axis=0, concat_axis=0, tiled=True)
    above, below = first_near(own[: 2 * NB], "z"), first_near(own[2 * NB :], "x")
    above = jnp.concatenate([above, second_near(above, "z")])
    below = jnp.concatenate([below, second_near(below, "x")])
    incoming, above, below = lax.optimization_barrier((incoming, above, below))
    above, below = first_near(above, "x"), first_near(below, "z")
    direct, turned = sums(incoming)
    direct, turned, above, below = lax.optimization_barrier((direct, turned, above, below))
    turned = lax.ppermute(turned, AXES, from_partner())
    direct = first_near(direct, "y")
    panels = above, second_near(above, "x"), below, second_near(below, "z")
    turned, direct = lax.optimization_barrier((turned, direct))
    turned = first_near(turned, "y")
    direct = direct, second_near(direct, "y")
    turned = turned, second_near(turned, "y")
    other, left = product_for_other(panels, direct, turned)
    theirs = lax.ppermute(other, AXES, TO_OTHER_CORE)
    mine, owned = product_for_me(panels, left)
    product = mine + theirs
    potential_blocks = owned.reshape(4, 1, 2, 1, NB, NB)
    return potential_blocks, jnp.swapaxes(product, 1, 2).reshape(2, 1, NB, 2, NB)


def solution(mesh):
    placed = (
        P(AXES, None, None, None),
        P(AXES, None),
        P(AXES),
        P(AXES, None, None),
        P(None, "dom", None, "col", None),
    )
    return jax.shard_map(
        shards,
        mesh=mesh,
        in_specs=placed,
        out_specs=(P(None, "dom", None, "col", None, None), P(None, "col", None, "dom", None)),
        check_vma=False,
    )
```

```python
import functools

import jax
import jax.numpy as jnp
from jax import lax
from jax.experimental import pallas as pl
from jax.experimental.pallas import tpu as pltpu
from jax.sharding import PartitionSpec as P

F32 = jnp.float32
BF16 = jnp.bfloat16
AXES = ("dom", "col")
NB = 128
LOC = 16
NBLK = 32
NDOM = 8
NCOL = 16
NDEV = NDOM * NCOL
HELD = 4 * NB
SUB = 8
TILES = NB // SUB
ROWS = NB + SUB
CHUNK = 64
TILE = 16
VMEM = pl.BlockSpec(memory_space=pltpu.VMEM)
HBM = pl.BlockSpec(memory_space=pltpu.HBM)
SMEM = pl.BlockSpec(memory_space=pltpu.SMEM)


def upper(strict):
    row = lax.broadcasted_iota(jnp.int32, (NB, NB), 0)
    col = lax.broadcasted_iota(jnp.int32, (NB, NB), 1)
    return row < col if strict else row <= col


def home(kind, col):
    return kind ^ (col & 1)


def message_kernel(
    start_ref, pairs_ref, potential_ref, orbitals_ref, out_ref,
    held, weighted, diagonal, outgoing, pairs, potential, sems, out_sem,
):
    step_rows = 2 * NB
    steps = LOC // 2
    small = [
        pltpu.make_async_copy(pairs_ref, pairs, sems.at[steps]),
        pltpu.make_async_copy(potential_ref, potential, sems.at[steps + 1]),
    ]
    copies = [
        pltpu.make_async_copy(
            orbitals_ref.at[pl.ds(k * step_rows, step_rows)], held.at[pl.ds(k * step_rows, step_rows)], sems.at[k]
        )
        for k in range(steps)
    ]
    for copy in small + copies:
        copy.start()
    start = start_ref[0]
    tail_row = lax.broadcasted_iota(jnp.int32, (SUB, NB), 0)
    my_lanes = lax.broadcasted_iota(jnp.int32, (SUB, NB), 1) // TILE == lax.rem(lax.axis_index("col"), NB // TILE)
    eye = upper(False) & ~upper(True)
    for copy in small:
        copy.wait()
    codes = pairs[0:1, :] * LOC + pairs[1:2, :]
    scale = potential[...]

    slots = {}

    def send(kind, near, col, block, extra=None, now=True):
        slot = slots.setdefault((kind, col), len(slots))
        if block is not None:
            outgoing[slot, 0:TILES] = block.reshape(TILES, SUB, NB).astype(BF16)
        if not now:
            return
        block_col = lax.rem(start + col, NBLK)
        half = block_col // LOC
        last = jnp.where((tail_row == 0) & my_lanes, (half + (0 if near else 2)).astype(F32), 0.0)
        if extra is not None:
            last = jnp.where(tail_row == half + 1, extra, last)
        outgoing[slot, TILES] = last.astype(BF16)
        column = lax.rem(block_col, NCOL)
        target = home(kind, column) * NCOL + column
        pltpu.make_async_copy(outgoing.at[slot], out_ref.at[target], out_sem).start()

    for right in range(steps):
        copies[right].wait()
        right_rows = pl.ds(right * step_rows, step_rows)
        right_side = held[right_rows, :]
        weighted[right_rows, :] = (right_side.astype(F32) * scale).astype(BF16)
        for left in range(right + 1):
            tile = lax.dot_general(
                weighted[pl.ds(left * step_rows, step_rows), :],
                right_side,
                (((1,), (1,)), ((), ())),
                preferred_element_type=F32,
            )
            for a in (2 * left, 2 * left + 1):
                for b in (2 * right, 2 * right + 1):
                    block = tile[(a % 2) * NB : (a % 2 + 1) * NB, (b % 2) * NB : (b % 2 + 1) * NB]
                    gap = b - a
                    if gap < 0:
                        continue
                    if gap == 0 and a < LOC // 2:
                        diagonal[a] = block
                    elif gap == 0:
                        low = a - LOC // 2
                        send(0, False, low, jnp.where(upper(False), diagonal[low], block))
                        extra = jnp.sum(jnp.where(eye, block, 0.0), axis=0, keepdims=True)
                        send(0, True, a, None, extra)
                    elif gap < LOC // 2:
                        send(gap, True, b, block)
                    elif gap == LOC // 2:
                        send(0, True, b, block, now=False)
                    else:
                        listed = jnp.max(jnp.where(codes == a * LOC + b, 1.0, 0.0), axis=1, keepdims=True)
                        send(LOC - gap, False, a, block * listed)
    pltpu.make_async_copy(outgoing, out_ref, out_sem).wait()


def in_hbm(value):
    return pltpu.with_memory_space_constraint(value, pltpu.HBM)


def messages(domain_start, margin_pairs, potential, orbitals):
    rows = LOC * NB
    grid_points = orbitals.shape[-1]
    return pl.pallas_call(
        message_kernel,
        out_shape=pltpu.HBM((NDEV, TILES + 1, SUB, NB), BF16),
        in_specs=[SMEM, HBM, HBM, HBM],
        out_specs=HBM,
        scratch_shapes=[
            pltpu.VMEM((rows, grid_points), BF16),
            pltpu.VMEM((rows, grid_points), BF16),
            pltpu.VMEM((LOC // 2, NB, NB), F32),
            pltpu.VMEM((NDEV, TILES + 1, SUB, NB), BF16),
            pltpu.VMEM(margin_pairs.shape, jnp.int32),
            pltpu.VMEM(potential.shape, F32),
            pltpu.SemaphoreType.DMA((LOC // 2 + 2,)),
            pltpu.SemaphoreType.DMA,
        ],
        compiler_params=pltpu.CompilerParams(vmem_limit_bytes=40 << 20),
        cost_estimate=pl.CostEstimate(flops=5_000_000_000, bytes_accessed=9_000_000, transcendentals=0),
        name="blocks",
    )(domain_start, in_hbm(margin_pairs), in_hbm(potential), in_hbm(orbitals.reshape(rows, grid_points))).reshape(NDEV, ROWS, NB)


def wrap(value, size):
    return lax.rem(value + 2 * size, size)


def place():
    dom, col = lax.axis_index("dom"), lax.axis_index("col")
    return dom, col, home(dom, col)


def sum_kernel(in_ref, direct_ref, turned_ref, total, extra_total):
    step = pl.program_id(0)

    @pl.when(step == 0)
    def _():
        total[...] = jnp.zeros_like(total)
        extra_total[...] = jnp.zeros_like(extra_total)

    depth = CHUNK * TILE
    group = NB // TILE
    lasts = [jnp.sum(in_ref[m : m + group, NB:ROWS, :].astype(F32), axis=0) for m in range(0, CHUNK, group)]
    extra_total[...] += sum(lasts)
    lane_key = jnp.concatenate([last[0:1, :] for last in lasts], axis=1).astype(jnp.int32)
    row = lax.broadcasted_iota(jnp.int32, (4 * TILE, depth), 0)
    lane = lax.broadcasted_iota(jnp.int32, (4 * TILE, depth), 1)
    chosen = jnp.where((row // TILE == lane_key) & ((row & (TILE - 1)) == (lane & (TILE - 1))), 1.0, 0.0).astype(BF16)
    for pair in range(NB // TILE // 2):
        first = pair * 2 * TILE
        sides = [in_ref[:, first + t * TILE : first + (t + 1) * TILE, :].reshape(depth, NB) for t in range(2)]
        total[:, pair * 2 * NB : (pair + 1) * 2 * NB] += jnp.dot(
            chosen, jnp.concatenate(sides, axis=1), preferred_element_type=F32
        )

    @pl.when(step == NDEV // CHUNK - 1)
    def _():
        eye = upper(False) & ~upper(True)
        for k in range(4):
            plain = jnp.concatenate(
                [total[k * TILE : (k + 1) * TILE, t * NB : (t + 1) * NB] for t in range(NB // TILE)], axis=0
            )
            if k >= 2:
                plain = plain + jnp.where(eye, extra_total[k - 1 : k, :], 0.0)
            flipped = plain.T
            rows = pl.ds(k * NB, NB)
            direct_ref[rows, :] = (flipped if k < 2 else plain).astype(BF16)
            turned_ref[rows, :] = (plain if k < 2 else flipped).astype(BF16)


def sums(incoming):
    shape = jax.ShapeDtypeStruct((HELD, NB), BF16)
    return pl.pallas_call(
        sum_kernel,
        out_shape=(shape, shape),
        grid=(NDEV // CHUNK,),
        in_specs=[pl.BlockSpec((CHUNK, ROWS, NB), lambda i: (i, 0, 0))],
        out_specs=(pl.BlockSpec((HELD, NB), lambda i: (0, 0)),) * 2,
        scratch_shapes=[pltpu.VMEM((4 * TILE, NB // TILE * NB), F32), pltpu.VMEM((SUB, NB), F32)],
        cost_estimate=pl.CostEstimate(flops=300_000_000, bytes_accessed=4_700_000, transcendentals=0),
        name="sums",
    )(incoming)


def diagonal_block(col, half, direct, turned):
    other = lax.rem(col + LOC * half + NBLK - NDOM, NBLK) // LOC
    first = direct[pl.ds((2 + half) * NB, NB), :].astype(F32)
    second = turned[pl.ds(pl.multiple_of((2 + other) * NB, NB), NB), :].astype(F32)
    above = jnp.where(upper(True), first + second, 0.0)
    eye = upper(False) & ~upper(True)
    return jnp.where(eye, first, above + above.T)


def column_blocks(kind, col, direct, turned, put):
    near = jnp.where(kind == 0, LOC // 2, kind)
    other_col = lax.rem(col + near, NCOL)
    for half in range(2):
        mine = col + LOC * half
        theirs = other_col + LOC * half
        put(wrap(mine - near, NBLK), half, direct[pl.ds(half * NB, NB), :])
        put(theirs, wrap(theirs - near, NBLK) // LOC, turned[pl.ds(half * NB, NB), :])

    @pl.when(kind > 0)
    def _():
        for half in range(2):
            mine = col + LOC * half
            theirs = other_col + LOC * half
            rows = pl.ds((2 + half) * NB, NB)
            put(wrap(mine + LOC - kind, NBLK), half, direct[rows, :])
            put(theirs, wrap(theirs + LOC - kind, NBLK) // LOC, turned[rows, :])

    @pl.when(kind == 0)
    def _():
        for half in range(2):
            mine = col + LOC * half
            put(mine, half, diagonal_block(col, half, direct, turned).astype(BF16))
            put(wrap(mine + LOC, NBLK), half, jnp.zeros((NB, NB), BF16))


def ring_place(place_on_ring, core, k):
    even = jnp.where(lax.rem(place_on_ring, 2) == 0, place_on_ring + 1, place_on_ring - 1)
    odd = 3 - place_on_ring
    first, second = jnp.where(core == 0, even, odd), jnp.where(core == 0, odd, even)
    return (place_on_ring, first, second, wrap(place_on_ring + 2, 4))[k]


def half_product(panels, left, core, z, x, wanted, out_ref):
    upper_panel, lower_panel = panels[0:2], panels[2:4]
    depth = 2 * NB

    def add_up(steps):
        part = jnp.zeros((2 * NB, 2 * NB), F32)
        for z_step in range(4):
            start = pl.multiple_of(wrap(ring_place(z, core, z_step) + 2, 4) * (2 * depth), depth)
            above = [upper_panel[k // 2][k % 2, z_step] for k in steps]
            below = [lower_panel[z_step // 2][z_step % 2, k] for k in steps]
            part = part + jnp.dot(
                left[:, pl.ds(start, depth)], jnp.concatenate(above, axis=1), preferred_element_type=F32
            )
            part = part + jnp.dot(
                left[:, pl.ds(pl.multiple_of(start + depth, depth), depth)],
                jnp.concatenate(below, axis=1),
                preferred_element_type=F32,
            )
        for i, k in enumerate(steps):
            place_of = lax.rem(ring_place(x, core, k), 2)
            out_ref[:, place_of] = part[:, i * NB : (i + 1) * NB].reshape(2, NB, NB)

    near = wanted == x // 2
    for on, steps in (
        (near & (core == 0), (0, 1)),
        (~near & (core == 0), (2, 3)),
        (near & (core == 1), (0, 2)),
        (~near & (core == 1), (1, 3)),
    ):
        pl.when(on)(functools.partial(add_up, steps))


def other_kernel(*refs):
    panels, direct, turned = refs[0:4], refs[4:6], refs[6:8]
    other_ref, left = refs[8:10]
    dom, col, _ = place()
    y, core = dom // 2, lax.rem(dom, 2)

    def put(block_row, half, block):
        slot = (lax.rem(block_row, NDOM) // 2) * 4 + block_row // NDOM
        rows = pl.ds(half * NB if isinstance(half, int) else pl.multiple_of(half * NB, NB), NB)
        left[rows, pl.ds(pl.multiple_of(slot * NB, NB), NB)] = block

    for k in range(4):
        kind = home(2 * ring_place(y, core, k) + core, col)
        column_blocks(kind, col, direct[k // 2].at[k % 2], turned[k // 2].at[k % 2], put)
    half_product(panels, left, core, col // 4, lax.rem(col, 4), 1 - core, other_ref)


def mine_kernel(*refs):
    panels, left, mine_ref, blocks_ref = refs[0:4], refs[4], refs[5], refs[6]
    dom, col, _ = place()
    y, core = dom // 2, lax.rem(dom, 2)
    half_product(panels, left, core, col // 4, lax.rem(col, 4), core, mine_ref)
    for row in range(4):
        column = pl.ds(pl.multiple_of((y * 4 + row) * NB, NB), NB)
        for half in range(2):
            block = left[half * NB : (half + 1) * NB, column]
            blocks_ref[row, half] = block.astype(F32).T.astype(BF16)


def product_for_other(panels, direct, turned):
    return pl.pallas_call(
        other_kernel,
        out_shape=(jax.ShapeDtypeStruct((2, 2, NB, NB), F32), jax.ShapeDtypeStruct((2 * NB, 16 * NB), BF16)),
        in_specs=[VMEM] * 8,
        out_specs=(VMEM, VMEM),
        compiler_params=pltpu.CompilerParams(vmem_limit_bytes=32 << 20),
        cost_estimate=pl.CostEstimate(flops=270_000_000, bytes_accessed=4_000_000, transcendentals=0),
        name="other",
    )(*panels, *direct, *turned)


def product_for_me(panels, left):
    return pl.pallas_call(
        mine_kernel,
        out_shape=(jax.ShapeDtypeStruct((2, 2, NB, NB), F32), jax.ShapeDtypeStruct((4, 2, NB, NB), BF16)),
        in_specs=[VMEM] * 5,
        out_specs=(VMEM, VMEM),
        compiler_params=pltpu.CompilerParams(vmem_limit_bytes=32 << 20),
        cost_estimate=pl.CostEstimate(flops=270_000_000, bytes_accessed=4_000_000, transcendentals=0),
        name="mine",
    )(*panels, left)


def device(y, core, col):
    return (2 * y + core) * NCOL + col


PLACES = [(y, core, col) for y in range(4) for core in range(2) for col in range(NCOL)]
TO_ROW = [(device(y, core, col), device(col // 4, core, (y + 2) % 4 * 4 + col % 4)) for y, core, col in PLACES]
TO_OTHER_CORE = [(device(y, core, col), device(y, 1 - core, col)) for y, core, col in PLACES]


def from_partner():
    pairs = []
    for kind in range(NDOM):
        for col in range(NCOL):
            source = (col + (kind or LOC // 2)) % NCOL
            pairs.append((home(kind, source) * NCOL + source, home(kind, col) * NCOL + col))
    return pairs


def exchange(axis, step):
    pairs = []
    for y, core, col in PLACES:
        at = dict(y=y, z=col // 4, x=col % 4)
        at[axis] = at[axis] ^ 1 if core == step else 3 - at[axis]
        pairs.append((device(y, core, col), device(at["y"], core, 4 * at["z"] + at["x"])))
    return pairs


def first_near(value, axis):
    return jnp.stack([value, lax.ppermute(value, AXES, exchange(axis, 0))])


def second_near(pair, axis):
    return lax.ppermute(pair, AXES, exchange(axis, 1))


def shards(orbitals, potential, domain_start, margin_pairs, coefficients):
    own = lax.ppermute(coefficients.reshape(4 * NB, NB), AXES, TO_ROW)
    outgoing = messages(domain_start, margin_pairs[0], potential, orbitals)
    outgoing, own = lax.optimization_barrier((outgoing, own))
    incoming = lax.all_to_all(outgoing, AXES, split_axis=0, concat_axis=0, tiled=True)
    above, below = first_near(own[: 2 * NB], "z"), first_near(own[2 * NB :], "x")
    above = jnp.concatenate([above, second_near(above, "z")])
    below = jnp.concatenate([below, second_near(below, "x")])
    incoming, above, below = lax.optimization_barrier((incoming, above, below))
    above, below = first_near(above, "x"), first_near(below, "z")
    direct, turned = sums(incoming)
    direct, turned, above, below = lax.optimization_barrier((direct, turned, above, below))
    turned = lax.ppermute(turned, AXES, from_partner())
    direct = first_near(direct, "y")
    panels = above, second_near(above, "x"), below, second_near(below, "z")
    turned, direct = lax.optimization_barrier((turned, direct))
    turned = first_near(turned, "y")
    direct = direct, second_near(direct, "y")
    turned = turned, second_near(turned, "y")
    other, left = product_for_other(panels, direct, turned)
    theirs = lax.ppermute(other, AXES, TO_OTHER_CORE)
    mine, owned = product_for_me(panels, left)
    product = mine + theirs
    potential_blocks = owned.reshape(4, 1, 2, 1, NB, NB)
    return potential_blocks, jnp.swapaxes(product, 1, 2).reshape(2, 1, NB, 2, NB)


def solution(mesh):
    placed = (
        P(AXES, None, None, None),
        P(AXES, None),
        P(AXES),
        P(AXES, None, None),
        P(None, "dom", None, "col", None),
    )
    return jax.shard_map(
        shards,
        mesh=mesh,
        in_specs=placed,
        out_specs=(P(None, "dom", None, "col", None, None), P(None, "col", None, "dom", None)),
        check_vma=False,
    )
```

```python
import functools

import jax
import jax.numpy as jnp
from jax import lax
from jax.experimental import pallas as pl
from jax.experimental.pallas import tpu as pltpu
from jax.sharding import PartitionSpec as P

F32 = jnp.float32
BF16 = jnp.bfloat16
AXES = ("dom", "col")
NB = 128
LOC = 16
NBLK = 32
NDOM = 8
NCOL = 16
NDEV = NDOM * NCOL
HELD = 4 * NB
SUB = 8
TILES = NB // SUB
ROWS = NB + SUB
CHUNK = 64
TILE = 16
VMEM = pl.BlockSpec(memory_space=pltpu.VMEM)
HBM = pl.BlockSpec(memory_space=pltpu.HBM)
SMEM = pl.BlockSpec(memory_space=pltpu.SMEM)


def upper(strict):
    row = lax.broadcasted_iota(jnp.int32, (NB, NB), 0)
    col = lax.broadcasted_iota(jnp.int32, (NB, NB), 1)
    return row < col if strict else row <= col


def home(kind, col):
    return kind ^ (col & 1)


def message_kernel(
    start_ref, pairs_ref, potential_ref, orbitals_ref, out_ref,
    held, weighted, diagonal, outgoing, pairs, potential, sems, out_sem,
):
    step_rows = 2 * NB
    steps = LOC // 2
    small = [
        pltpu.make_async_copy(pairs_ref, pairs, sems.at[steps]),
        pltpu.make_async_copy(potential_ref, potential, sems.at[steps + 1]),
    ]
    copies = [
        pltpu.make_async_copy(
            orbitals_ref.at[pl.ds(k * step_rows, step_rows)], held.at[pl.ds(k * step_rows, step_rows)], sems.at[k]
        )
        for k in range(steps)
    ]
    for copy in small + copies:
        copy.start()
    start = start_ref[0]
    tail_row = lax.broadcasted_iota(jnp.int32, (SUB, NB), 0)
    my_lanes = lax.broadcasted_iota(jnp.int32, (SUB, NB), 1) // TILE == lax.rem(lax.axis_index("col"), NB // TILE)
    eye = upper(False) & ~upper(True)
    for copy in small:
        copy.wait()
    codes = pairs[0:1, :] * LOC + pairs[1:2, :]
    scale = potential[...]

    slots = {}

    def send(kind, near, col, block, extra=None, now=True):
        slot = slots.setdefault((kind, col), len(slots))
        if block is not None:
            outgoing[slot, 0:TILES] = block.reshape(TILES, SUB, NB).astype(BF16)
        if not now:
            return
        block_col = lax.rem(start + col, NBLK)
        half = block_col // LOC
        last = jnp.where((tail_row == 0) & my_lanes, (half + (0 if near else 2)).astype(F32), 0.0)
        if extra is not None:
            last = jnp.where(tail_row == half + 1, extra, last)
        outgoing[slot, TILES] = last.astype(BF16)
        column = lax.rem(block_col, NCOL)
        target = home(kind, column) * NCOL + column
        pltpu.make_async_copy(outgoing.at[slot], out_ref.at[target], out_sem).start()

    wide = 2 * step_rows
    for right in range(steps // 2):
        for half_step in (2 * right, 2 * right + 1):
            copies[half_step].wait()
            rows = pl.ds(half_step * step_rows, step_rows)
            weighted[rows, :] = (held[rows, :].astype(F32) * scale).astype(BF16)
        for left in range(2 * right + 2):
            tile = lax.dot_general(
                weighted[pl.ds(left * step_rows, step_rows), :],
                held[pl.ds(right * wide, wide), :],
                (((1,), (1,)), ((), ())),
                preferred_element_type=F32,
            )
            for a in (2 * left, 2 * left + 1):
                for b in range(4 * right, 4 * right + 4):
                    block = tile[(a % 2) * NB : (a % 2 + 1) * NB, (b % 4) * NB : (b % 4 + 1) * NB]
                    gap = b - a
                    if gap < 0:
                        continue
                    if gap == 0 and a < LOC // 2:
                        diagonal[a] = block
                    elif gap == 0:
                        low = a - LOC // 2
                        send(0, False, low, jnp.where(upper(False), diagonal[low], block))
                        extra = jnp.sum(jnp.where(eye, block, 0.0), axis=0, keepdims=True)
                        send(0, True, a, None, extra)
                    elif gap < LOC // 2:
                        send(gap, True, b, block)
                    elif gap == LOC // 2:
                        send(0, True, b, block, now=False)
                    else:
                        listed = jnp.max(jnp.where(codes == a * LOC + b, 1.0, 0.0), axis=1, keepdims=True)
                        send(LOC - gap, False, a, block * listed)
    pltpu.make_async_copy(outgoing, out_ref, out_sem).wait()


def in_hbm(value):
    return pltpu.with_memory_space_constraint(value, pltpu.HBM)


def messages(domain_start, margin_pairs, potential, orbitals):
    rows = LOC * NB
    grid_points = orbitals.shape[-1]
    return pl.pallas_call(
        message_kernel,
        out_shape=pltpu.HBM((NDEV, TILES + 1, SUB, NB), BF16),
        in_specs=[SMEM, HBM, HBM, HBM],
        out_specs=HBM,
        scratch_shapes=[
            pltpu.VMEM((rows, grid_points), BF16),
            pltpu.VMEM((rows, grid_points), BF16),
            pltpu.VMEM((LOC // 2, NB, NB), F32),
            pltpu.VMEM((NDEV, TILES + 1, SUB, NB), BF16),
            pltpu.VMEM(margin_pairs.shape, jnp.int32),
            pltpu.VMEM(potential.shape, F32),
            pltpu.SemaphoreType.DMA((LOC // 2 + 2,)),
            pltpu.SemaphoreType.DMA,
        ],
        compiler_params=pltpu.CompilerParams(vmem_limit_bytes=40 << 20),
        cost_estimate=pl.CostEstimate(flops=5_000_000_000, bytes_accessed=9_000_000, transcendentals=0),
        name="blocks",
    )(domain_start, in_hbm(margin_pairs), in_hbm(potential), in_hbm(orbitals.reshape(rows, grid_points))).reshape(NDEV, ROWS, NB)


def wrap(value, size):
    return lax.rem(value + 2 * size, size)


def place():
    dom, col = lax.axis_index("dom"), lax.axis_index("col")
    return dom, col, home(dom, col)


def sum_kernel(in_ref, direct_ref, turned_ref, total, extra_total):
    step = pl.program_id(0)

    @pl.when(step == 0)
    def _():
        total[...] = jnp.zeros_like(total)
        extra_total[...] = jnp.zeros_like(extra_total)

    depth = CHUNK * TILE
    group = NB // TILE
    lasts = [jnp.sum(in_ref[m : m + group, NB:ROWS, :].astype(F32), axis=0) for m in range(0, CHUNK, group)]
    extra_total[...] += sum(lasts)
    lane_key = jnp.concatenate([last[0:1, :] for last in lasts], axis=1).astype(jnp.int32)
    row = lax.broadcasted_iota(jnp.int32, (4 * TILE, depth), 0)
    lane = lax.broadcasted_iota(jnp.int32, (4 * TILE, depth), 1)
    chosen = jnp.where((row // TILE == lane_key) & ((row & (TILE - 1)) == (lane & (TILE - 1))), 1.0, 0.0).astype(BF16)
    for pair in range(NB // TILE // 2):
        first = pair * 2 * TILE
        sides = [in_ref[:, first + t * TILE : first + (t + 1) * TILE, :].reshape(depth, NB) for t in range(2)]
        total[:, pair * 2 * NB : (pair + 1) * 2 * NB] += jnp.dot(
            chosen, jnp.concatenate(sides, axis=1), preferred_element_type=F32
        )

    @pl.when(step == NDEV // CHUNK - 1)
    def _():
        eye = upper(False) & ~upper(True)
        for k in range(4):
            plain = jnp.concatenate(
                [total[k * TILE : (k + 1) * TILE, t * NB : (t + 1) * NB] for t in range(NB // TILE)], axis=0
            )
            if k >= 2:
                plain = plain + jnp.where(eye, extra_total[k - 1 : k, :], 0.0)
            flipped = plain.T
            rows = pl.ds(k * NB, NB)
            direct_ref[rows, :] = (flipped if k < 2 else plain).astype(BF16)
            turned_ref[rows, :] = (plain if k < 2 else flipped).astype(BF16)


def sums(incoming):
    shape = jax.ShapeDtypeStruct((HELD, NB), BF16)
    return pl.pallas_call(
        sum_kernel,
        out_shape=(shape, shape),
        grid=(NDEV // CHUNK,),
        in_specs=[pl.BlockSpec((CHUNK, ROWS, NB), lambda i: (i, 0, 0))],
        out_specs=(pl.BlockSpec((HELD, NB), lambda i: (0, 0)),) * 2,
        scratch_shapes=[pltpu.VMEM((4 * TILE, NB // TILE * NB), F32), pltpu.VMEM((SUB, NB), F32)],
        cost_estimate=pl.CostEstimate(flops=300_000_000, bytes_accessed=4_700_000, transcendentals=0),
        name="sums",
    )(incoming)


def diagonal_block(col, half, direct, turned):
    other = lax.rem(col + LOC * half + NBLK - NDOM, NBLK) // LOC
    first = direct[pl.ds((2 + half) * NB, NB), :].astype(F32)
    second = turned[pl.ds(pl.multiple_of((2 + other) * NB, NB), NB), :].astype(F32)
    above = jnp.where(upper(True), first + second, 0.0)
    eye = upper(False) & ~upper(True)
    return jnp.where(eye, first, above + above.T)


def column_blocks(kind, col, direct, turned, put):
    near = jnp.where(kind == 0, LOC // 2, kind)
    other_col = lax.rem(col + near, NCOL)
    for half in range(2):
        mine = col + LOC * half
        theirs = other_col + LOC * half
        put(wrap(mine - near, NBLK), half, direct[pl.ds(half * NB, NB), :])
        put(theirs, wrap(theirs - near, NBLK) // LOC, turned[pl.ds(half * NB, NB), :])

    @pl.when(kind > 0)
    def _():
        for half in range(2):
            mine = col + LOC * half
            theirs = other_col + LOC * half
            rows = pl.ds((2 + half) * NB, NB)
            put(wrap(mine + LOC - kind, NBLK), half, direct[rows, :])
            put(theirs, wrap(theirs + LOC - kind, NBLK) // LOC, turned[rows, :])

    @pl.when(kind == 0)
    def _():
        for half in range(2):
            mine = col + LOC * half
            put(mine, half, diagonal_block(col, half, direct, turned).astype(BF16))
            put(wrap(mine + LOC, NBLK), half, jnp.zeros((NB, NB), BF16))


def ring_place(place_on_ring, core, k):
    even = jnp.where(lax.rem(place_on_ring, 2) == 0, place_on_ring + 1, place_on_ring - 1)
    odd = 3 - place_on_ring
    first, second = jnp.where(core == 0, even, odd), jnp.where(core == 0, odd, even)
    return (place_on_ring, first, second, wrap(place_on_ring + 2, 4))[k]


def half_product(panels, left, core, z, x, wanted, out_ref):
    upper_panel, lower_panel = panels[0:2], panels[2:4]
    depth = 2 * NB

    def add_up(steps):
        part = jnp.zeros((2 * NB, 2 * NB), F32)
        for z_step in range(4):
            start = pl.multiple_of(wrap(ring_place(z, core, z_step) + 2, 4) * (2 * depth), depth)
            above = [upper_panel[k // 2][k % 2, z_step] for k in steps]
            below = [lower_panel[z_step // 2][z_step % 2, k] for k in steps]
            part = part + jnp.dot(
                left[:, pl.ds(start, depth)], jnp.concatenate(above, axis=1), preferred_element_type=F32
            )
            part = part + jnp.dot(
                left[:, pl.ds(pl.multiple_of(start + depth, depth), depth)],
                jnp.concatenate(below, axis=1),
                preferred_element_type=F32,
            )
        for i, k in enumerate(steps):
            place_of = lax.rem(ring_place(x, core, k), 2)
            out_ref[:, place_of] = part[:, i * NB : (i + 1) * NB].reshape(2, NB, NB)

    near = wanted == x // 2
    for on, steps in (
        (near & (core == 0), (0, 1)),
        (~near & (core == 0), (2, 3)),
        (near & (core == 1), (0, 2)),
        (~near & (core == 1), (1, 3)),
    ):
        pl.when(on)(functools.partial(add_up, steps))


def other_kernel(*refs):
    panels, direct, turned = refs[0:4], refs[4:6], refs[6:8]
    other_ref, left = refs[8:10]
    dom, col, _ = place()
    y, core = dom // 2, lax.rem(dom, 2)

    def put(block_row, half, block):
        slot = (lax.rem(block_row, NDOM) // 2) * 4 + block_row // NDOM
        rows = pl.ds(half * NB if isinstance(half, int) else pl.multiple_of(half * NB, NB), NB)
        left[rows, pl.ds(pl.multiple_of(slot * NB, NB), NB)] = block

    for k in range(4):
        kind = home(2 * ring_place(y, core, k) + core, col)
        column_blocks(kind, col, direct[k // 2].at[k % 2], turned[k // 2].at[k % 2], put)
    half_product(panels, left, core, col // 4, lax.rem(col, 4), 1 - core, other_ref)


def mine_kernel(*refs):
    panels, left, mine_ref, blocks_ref = refs[0:4], refs[4], refs[5], refs[6]
    dom, col, _ = place()
    y, core = dom // 2, lax.rem(dom, 2)
    half_product(panels, left, core, col // 4, lax.rem(col, 4), core, mine_ref)
    for row in range(4):
        column = pl.ds(pl.multiple_of((y * 4 + row) * NB, NB), NB)
        for half in range(2):
            block = left[half * NB : (half + 1) * NB, column]
            blocks_ref[row, half] = block.astype(F32).T.astype(BF16)


def product_for_other(panels, direct, turned):
    return pl.pallas_call(
        other_kernel,
        out_shape=(jax.ShapeDtypeStruct((2, 2, NB, NB), F32), jax.ShapeDtypeStruct((2 * NB, 16 * NB), BF16)),
        in_specs=[VMEM] * 8,
        out_specs=(VMEM, VMEM),
        compiler_params=pltpu.CompilerParams(vmem_limit_bytes=32 << 20),
        cost_estimate=pl.CostEstimate(flops=270_000_000, bytes_accessed=4_000_000, transcendentals=0),
        name="other",
    )(*panels, *direct, *turned)


def product_for_me(panels, left):
    return pl.pallas_call(
        mine_kernel,
        out_shape=(jax.ShapeDtypeStruct((2, 2, NB, NB), F32), jax.ShapeDtypeStruct((4, 2, NB, NB), BF16)),
        in_specs=[VMEM] * 5,
        out_specs=(VMEM, VMEM),
        compiler_params=pltpu.CompilerParams(vmem_limit_bytes=32 << 20),
        cost_estimate=pl.CostEstimate(flops=270_000_000, bytes_accessed=4_000_000, transcendentals=0),
        name="mine",
    )(*panels, left)


def device(y, core, col):
    return (2 * y + core) * NCOL + col


PLACES = [(y, core, col) for y in range(4) for core in range(2) for col in range(NCOL)]
TO_ROW = [(device(y, core, col), device(col // 4, core, (y + 2) % 4 * 4 + col % 4)) for y, core, col in PLACES]
TO_OTHER_CORE = [(device(y, core, col), device(y, 1 - core, col)) for y, core, col in PLACES]


def from_partner():
    pairs = []
    for kind in range(NDOM):
        for col in range(NCOL):
            source = (col + (kind or LOC // 2)) % NCOL
            pairs.append((home(kind, source) * NCOL + source, home(kind, col) * NCOL + col))
    return pairs


def exchange(axis, step):
    pairs = []
    for y, core, col in PLACES:
        at = dict(y=y, z=col // 4, x=col % 4)
        at[axis] = at[axis] ^ 1 if core == step else 3 - at[axis]
        pairs.append((device(y, core, col), device(at["y"], core, 4 * at["z"] + at["x"])))
    return pairs


def first_near(value, axis):
    return jnp.stack([value, lax.ppermute(value, AXES, exchange(axis, 0))])


def second_near(pair, axis):
    return lax.ppermute(pair, AXES, exchange(axis, 1))


def shards(orbitals, potential, domain_start, margin_pairs, coefficients):
    own = lax.ppermute(coefficients.reshape(4 * NB, NB), AXES, TO_ROW)
    outgoing = messages(domain_start, margin_pairs[0], potential, orbitals)
    outgoing, own = lax.optimization_barrier((outgoing, own))
    incoming = lax.all_to_all(outgoing, AXES, split_axis=0, concat_axis=0, tiled=True)
    above, below = first_near(own[: 2 * NB], "z"), first_near(own[2 * NB :], "x")
    above = jnp.concatenate([above, second_near(above, "z")])
    below = jnp.concatenate([below, second_near(below, "x")])
    incoming, above, below = lax.optimization_barrier((incoming, above, below))
    above, below = first_near(above, "x"), first_near(below, "z")
    direct, turned = sums(incoming)
    direct, turned, above, below = lax.optimization_barrier((direct, turned, above, below))
    turned = lax.ppermute(turned, AXES, from_partner())
    direct = first_near(direct, "y")
    panels = above, second_near(above, "x"), below, second_near(below, "z")
    turned = first_near(turned, "y")
    direct = direct, second_near(direct, "y")
    turned = turned, second_near(turned, "y")
    other, left = product_for_other(panels, direct, turned)
    theirs = lax.ppermute(other, AXES, TO_OTHER_CORE)
    mine, owned = product_for_me(panels, left)
    product = mine + theirs
    potential_blocks = owned.reshape(4, 1, 2, 1, NB, NB)
    return potential_blocks, jnp.swapaxes(product, 1, 2).reshape(2, 1, NB, 2, NB)


def solution(mesh):
    placed = (
        P(AXES, None, None, None),
        P(AXES, None),
        P(AXES),
        P(AXES, None, None),
        P(None, "dom", None, "col", None),
    )
    return jax.shard_map(
        shards,
        mesh=mesh,
        in_specs=placed,
        out_specs=(P(None, "dom", None, "col", None, None), P(None, "col", None, "dom", None)),
        check_vma=False,
    )
```

```python
import functools

import jax
import jax.numpy as jnp
from jax import lax
from jax.experimental import pallas as pl
from jax.experimental.pallas import tpu as pltpu
from jax.sharding import PartitionSpec as P

F32 = jnp.float32
BF16 = jnp.bfloat16
AXES = ("dom", "col")
NB = 128
LOC = 16
NBLK = 32
NDOM = 8
NCOL = 16
NDEV = NDOM * NCOL
HELD = 4 * NB
SUB = 8
TILES = NB // SUB
ROWS = NB + SUB
CHUNK = 64
TILE = 16
VMEM = pl.BlockSpec(memory_space=pltpu.VMEM)
HBM = pl.BlockSpec(memory_space=pltpu.HBM)
SMEM = pl.BlockSpec(memory_space=pltpu.SMEM)


def upper(strict):
    row = lax.broadcasted_iota(jnp.int32, (NB, NB), 0)
    col = lax.broadcasted_iota(jnp.int32, (NB, NB), 1)
    return row < col if strict else row <= col


def home(kind, col):
    return kind ^ (col & 1)


def message_kernel(
    start_ref, pairs_ref, potential_ref, orbitals_ref, out_ref,
    held, weighted, diagonal, outgoing, pairs, potential, sems, out_sem,
):
    step_rows = 2 * NB
    steps = LOC // 2
    small = [
        pltpu.make_async_copy(pairs_ref, pairs, sems.at[steps]),
        pltpu.make_async_copy(potential_ref, potential, sems.at[steps + 1]),
    ]
    copies = [
        pltpu.make_async_copy(
            orbitals_ref.at[pl.ds(k * step_rows, step_rows)], held.at[pl.ds(k * step_rows, step_rows)], sems.at[k]
        )
        for k in range(steps)
    ]
    for copy in small + copies:
        copy.start()
    start = start_ref[0]
    tail_row = lax.broadcasted_iota(jnp.int32, (SUB, NB), 0)
    my_lanes = lax.broadcasted_iota(jnp.int32, (SUB, NB), 1) // TILE == lax.rem(lax.axis_index("col"), NB // TILE)
    eye = upper(False) & ~upper(True)
    for copy in small:
        copy.wait()
    codes = pairs[0:1, :] * LOC + pairs[1:2, :]
    scale = potential[...]

    slots = {}

    def send(kind, near, col, block, extra=None, now=True):
        slot = slots.setdefault((kind, col), len(slots))
        if block is not None:
            outgoing[slot, 0:TILES] = block.reshape(TILES, SUB, NB).astype(BF16)
        if not now:
            return
        block_col = lax.rem(start + col, NBLK)
        half = block_col // LOC
        last = jnp.where((tail_row == 0) & my_lanes, (half + (0 if near else 2)).astype(F32), 0.0)
        if extra is not None:
            last = jnp.where(tail_row == half + 1, extra, last)
        outgoing[slot, TILES] = last.astype(BF16)
        column = lax.rem(block_col, NCOL)
        target = home(kind, column) * NCOL + column
        pltpu.make_async_copy(outgoing.at[slot], out_ref.at[target], out_sem).start()

    wide = 2 * step_rows
    for right in range(steps // 2):
        for half_step in (2 * right, 2 * right + 1):
            copies[half_step].wait()
            rows = pl.ds(half_step * step_rows, step_rows)
            weighted[rows, :] = (held[rows, :].astype(F32) * scale).astype(BF16)
        for left in range(2 * right + 2):
            tile = lax.dot_general(
                weighted[pl.ds(left * step_rows, step_rows), :],
                held[pl.ds(right * wide, wide), :],
                (((1,), (1,)), ((), ())),
                preferred_element_type=F32,
            )
            for a in (2 * left, 2 * left + 1):
                for b in range(4 * right, 4 * right + 4):
                    block = tile[(a % 2) * NB : (a % 2 + 1) * NB, (b % 4) * NB : (b % 4 + 1) * NB]
                    gap = b - a
                    if gap < 0:
                        continue
                    if gap == 0 and a < LOC // 2:
                        diagonal[a] = block
                    elif gap == 0:
                        low = a - LOC // 2
                        send(0, False, low, jnp.where(upper(False), diagonal[low], block))
                        extra = jnp.sum(jnp.where(eye, block, 0.0), axis=0, keepdims=True)
                        send(0, True, a, None, extra)
                    elif gap < LOC // 2:
                        send(gap, True, b, block)
                    elif gap == LOC // 2:
                        send(0, True, b, block, now=False)
                    else:
                        listed = jnp.max(jnp.where(codes == a * LOC + b, 1.0, 0.0), axis=1, keepdims=True)
                        send(LOC - gap, False, a, block * listed)
    pltpu.make_async_copy(outgoing, out_ref, out_sem).wait()


def in_hbm(value):
    return pltpu.with_memory_space_constraint(value, pltpu.HBM)


def messages(domain_start, margin_pairs, potential, orbitals):
    rows = LOC * NB
    grid_points = orbitals.shape[-1]
    return pl.pallas_call(
        message_kernel,
        out_shape=pltpu.HBM((NDEV, TILES + 1, SUB, NB), BF16),
        in_specs=[SMEM, HBM, HBM, HBM],
        out_specs=HBM,
        scratch_shapes=[
            pltpu.VMEM((rows, grid_points), BF16),
            pltpu.VMEM((rows, grid_points), BF16),
            pltpu.VMEM((LOC // 2, NB, NB), F32),
            pltpu.VMEM((NDEV, TILES + 1, SUB, NB), BF16),
            pltpu.VMEM(margin_pairs.shape, jnp.int32),
            pltpu.VMEM(potential.shape, F32),
            pltpu.SemaphoreType.DMA((LOC // 2 + 2,)),
            pltpu.SemaphoreType.DMA,
        ],
        compiler_params=pltpu.CompilerParams(vmem_limit_bytes=40 << 20),
        cost_estimate=pl.CostEstimate(flops=5_000_000_000, bytes_accessed=9_000_000, transcendentals=0),
        name="blocks",
    )(domain_start, in_hbm(margin_pairs), in_hbm(potential), in_hbm(orbitals.reshape(rows, grid_points))).reshape(NDEV, ROWS, NB)


def wrap(value, size):
    return lax.rem(value + 2 * size, size)


def place():
    dom, col = lax.axis_index("dom"), lax.axis_index("col")
    return dom, col, home(dom, col)


def sum_kernel(in_ref, direct_ref, turned_ref, total, extra_total):
    step = pl.program_id(0)

    @pl.when(step == 0)
    def _():
        total[...] = jnp.zeros_like(total)
        extra_total[...] = jnp.zeros_like(extra_total)

    depth = CHUNK * TILE
    group = NB // TILE
    lasts = [jnp.sum(in_ref[m : m + group, NB:ROWS, :].astype(F32), axis=0) for m in range(0, CHUNK, group)]
    extra_total[...] += sum(lasts)
    lane_key = jnp.concatenate([last[0:1, :] for last in lasts], axis=1).astype(jnp.int32)
    row = lax.broadcasted_iota(jnp.int32, (4 * TILE, depth), 0)
    lane = lax.broadcasted_iota(jnp.int32, (4 * TILE, depth), 1)
    chosen = jnp.where((row // TILE == lane_key) & ((row & (TILE - 1)) == (lane & (TILE - 1))), 1.0, 0.0).astype(BF16)
    for pair in range(NB // TILE // 2):
        first = pair * 2 * TILE
        sides = [in_ref[:, first + t * TILE : first + (t + 1) * TILE, :].reshape(depth, NB) for t in range(2)]
        total[:, pair * 2 * NB : (pair + 1) * 2 * NB] += jnp.dot(
            chosen, jnp.concatenate(sides, axis=1), preferred_element_type=F32
        )

    @pl.when(step == NDEV // CHUNK - 1)
    def _():
        eye = upper(False) & ~upper(True)
        for k in range(4):
            plain = jnp.concatenate(
                [total[k * TILE : (k + 1) * TILE, t * NB : (t + 1) * NB] for t in range(NB // TILE)], axis=0
            )
            if k >= 2:
                plain = plain + jnp.where(eye, extra_total[k - 1 : k, :], 0.0)
            flipped = plain.T
            rows = pl.ds(k * NB, NB)
            direct_ref[rows, :] = (flipped if k < 2 else plain).astype(BF16)
            turned_ref[rows, :] = (plain if k < 2 else flipped).astype(BF16)


def sums(incoming):
    shape = jax.ShapeDtypeStruct((HELD, NB), BF16)
    return pl.pallas_call(
        sum_kernel,
        out_shape=(shape, shape),
        grid=(NDEV // CHUNK,),
        in_specs=[pl.BlockSpec((CHUNK, ROWS, NB), lambda i: (i, 0, 0))],
        out_specs=(pl.BlockSpec((HELD, NB), lambda i: (0, 0)),) * 2,
        scratch_shapes=[pltpu.VMEM((4 * TILE, NB // TILE * NB), F32), pltpu.VMEM((SUB, NB), F32)],
        cost_estimate=pl.CostEstimate(flops=300_000_000, bytes_accessed=4_700_000, transcendentals=0),
        name="sums",
    )(incoming)


def diagonal_block(col, half, direct, turned):
    other = lax.rem(col + LOC * half + NBLK - NDOM, NBLK) // LOC
    first = direct[pl.ds((2 + half) * NB, NB), :].astype(F32)
    second = turned[pl.ds(pl.multiple_of((2 + other) * NB, NB), NB), :].astype(F32)
    above = jnp.where(upper(True), first + second, 0.0)
    eye = upper(False) & ~upper(True)
    return jnp.where(eye, first, above + above.T)


def column_blocks(kind, col, direct, turned, put):
    near = jnp.where(kind == 0, LOC // 2, kind)
    other_col = lax.rem(col + near, NCOL)
    for half in range(2):
        mine = col + LOC * half
        theirs = other_col + LOC * half
        put(wrap(mine - near, NBLK), half, direct[pl.ds(half * NB, NB), :])
        put(theirs, wrap(theirs - near, NBLK) // LOC, turned[pl.ds(half * NB, NB), :])

    @pl.when(kind > 0)
    def _():
        for half in range(2):
            mine = col + LOC * half
            theirs = other_col + LOC * half
            rows = pl.ds((2 + half) * NB, NB)
            put(wrap(mine + LOC - kind, NBLK), half, direct[rows, :])
            put(theirs, wrap(theirs + LOC - kind, NBLK) // LOC, turned[rows, :])

    @pl.when(kind == 0)
    def _():
        for half in range(2):
            mine = col + LOC * half
            put(mine, half, diagonal_block(col, half, direct, turned).astype(BF16))
            put(wrap(mine + LOC, NBLK), half, jnp.zeros((NB, NB), BF16))


def ring_place(place_on_ring, core, k):
    even = jnp.where(lax.rem(place_on_ring, 2) == 0, place_on_ring + 1, place_on_ring - 1)
    odd = 3 - place_on_ring
    first, second = jnp.where(core == 0, even, odd), jnp.where(core == 0, odd, even)
    return (place_on_ring, first, second, wrap(place_on_ring + 2, 4))[k]


def half_product(panels, left, y, core, z, x, wanted, out_ref):
    upper_panel, lower_panel = panels[0:2], panels[2:4]
    depth = 2 * NB

    def add_up(steps):
        part = jnp.zeros((2 * NB, 2 * NB), F32)
        for z_step in range(4):
            their_z = ring_place(z, core, z_step)
            their_y = wrap(jnp.where(core == 0, their_z, 2 * y - their_z) + 2, 4)
            start = pl.multiple_of(their_y * (2 * depth), depth)
            above = [upper_panel[k // 2][k % 2, z_step] for k in steps]
            below = [lower_panel[z_step // 2][z_step % 2, k] for k in steps]
            part = part + jnp.dot(
                left[:, pl.ds(start, depth)], jnp.concatenate(above, axis=1), preferred_element_type=F32
            )
            part = part + jnp.dot(
                left[:, pl.ds(pl.multiple_of(start + depth, depth), depth)],
                jnp.concatenate(below, axis=1),
                preferred_element_type=F32,
            )
        for i, k in enumerate(steps):
            place_of = lax.rem(ring_place(x, core, k), 2)
            out_ref[:, place_of] = part[:, i * NB : (i + 1) * NB].reshape(2, NB, NB)

    near = wanted == x // 2
    for on, steps in (
        (near & (core == 0), (0, 1)),
        (~near & (core == 0), (2, 3)),
        (near & (core == 1), (0, 2)),
        (~near & (core == 1), (1, 3)),
    ):
        pl.when(on)(functools.partial(add_up, steps))


def other_kernel(*refs):
    panels, direct, turned = refs[0:4], refs[4:6], refs[6:8]
    other_ref, left = refs[8:10]
    dom, col, _ = place()
    y, core = dom // 2, lax.rem(dom, 2)

    def put(block_row, half, block):
        slot = (lax.rem(block_row, NDOM) // 2) * 4 + block_row // NDOM
        rows = pl.ds(half * NB if isinstance(half, int) else pl.multiple_of(half * NB, NB), NB)
        left[rows, pl.ds(pl.multiple_of(slot * NB, NB), NB)] = block

    for k in range(4):
        kind = home(2 * ring_place(y, core, k) + core, col)
        column_blocks(kind, col, direct[k % 2].at[k // 2], turned[k // 2].at[k % 2], put)
    half_product(panels, left, y, core, col // 4, lax.rem(col, 4), 1 - core, other_ref)


def mine_kernel(*refs):
    panels, left, mine_ref, blocks_ref = refs[0:4], refs[4], refs[5], refs[6]
    dom, col, _ = place()
    y, core = dom // 2, lax.rem(dom, 2)
    half_product(panels, left, y, core, col // 4, lax.rem(col, 4), core, mine_ref)
    for row in range(4):
        column = pl.ds(pl.multiple_of((y * 4 + row) * NB, NB), NB)
        for half in range(2):
            block = left[half * NB : (half + 1) * NB, column]
            blocks_ref[row, half] = block.astype(F32).T.astype(BF16)


def product_for_other(panels, direct, turned):
    return pl.pallas_call(
        other_kernel,
        out_shape=(jax.ShapeDtypeStruct((2, 2, NB, NB), F32), jax.ShapeDtypeStruct((2 * NB, 16 * NB), BF16)),
        in_specs=[VMEM] * 8,
        out_specs=(VMEM, VMEM),
        compiler_params=pltpu.CompilerParams(vmem_limit_bytes=32 << 20),
        cost_estimate=pl.CostEstimate(flops=270_000_000, bytes_accessed=4_000_000, transcendentals=0),
        name="other",
    )(*panels, *direct, *turned)


def product_for_me(panels, left):
    return pl.pallas_call(
        mine_kernel,
        out_shape=(jax.ShapeDtypeStruct((2, 2, NB, NB), F32), jax.ShapeDtypeStruct((4, 2, NB, NB), BF16)),
        in_specs=[VMEM] * 5,
        out_specs=(VMEM, VMEM),
        compiler_params=pltpu.CompilerParams(vmem_limit_bytes=32 << 20),
        cost_estimate=pl.CostEstimate(flops=270_000_000, bytes_accessed=4_000_000, transcendentals=0),
        name="mine",
    )(*panels, left)


def device(y, core, col):
    return (2 * y + core) * NCOL + col


PLACES = [(y, core, col) for y in range(4) for core in range(2) for col in range(NCOL)]
TO_ROW = [
    (device(y, core, col), device(col // 4, core, ((2 * (col // 4) - y if core else y) + 2) % 4 * 4 + col % 4))
    for y, core, col in PLACES
]
TO_OTHER_CORE = [(device(y, core, col), device(y, 1 - core, col)) for y, core, col in PLACES]


def from_partner():
    pairs = []
    for kind in range(NDOM):
        for col in range(NCOL):
            source = (col + (kind or LOC // 2)) % NCOL
            pairs.append((home(kind, source) * NCOL + source, home(kind, col) * NCOL + col))
    return pairs


def exchange(axis, step):
    pairs = []
    for y, core, col in PLACES:
        at = dict(y=y, z=col // 4, x=col % 4)
        at[axis] = at[axis] ^ 1 if core == step else 3 - at[axis]
        pairs.append((device(y, core, col), device(at["y"], core, 4 * at["z"] + at["x"])))
    return pairs


def first_near(value, axis, step=0):
    return jnp.stack([value, lax.ppermute(value, AXES, exchange(axis, step))])


def second_near(pair, axis, step=1):
    return lax.ppermute(pair, AXES, exchange(axis, step))


def shards(orbitals, potential, domain_start, margin_pairs, coefficients):
    own = lax.ppermute(coefficients.reshape(4 * NB, NB), AXES, TO_ROW)
    outgoing = messages(domain_start, margin_pairs[0], potential, orbitals)
    outgoing, own = lax.optimization_barrier((outgoing, own))
    incoming = lax.all_to_all(outgoing, AXES, split_axis=0, concat_axis=0, tiled=True)
    above, below = first_near(own[: 2 * NB], "z"), first_near(own[2 * NB :], "x")
    above = jnp.concatenate([above, second_near(above, "z")])
    below = jnp.concatenate([below, second_near(below, "x")])
    incoming, above, below = lax.optimization_barrier((incoming, above, below))
    above, below = first_near(above, "x"), first_near(below, "z")
    direct, turned = sums(incoming)
    direct, turned, above, below = lax.optimization_barrier((direct, turned, above, below))
    turned = lax.ppermute(turned, AXES, from_partner())
    direct = first_near(direct, "y", 1)
    panels = above, second_near(above, "x"), below, second_near(below, "z")
    turned = first_near(turned, "y")
    direct = direct, second_near(direct, "y", 0)
    turned = turned, second_near(turned, "y")
    other, left = product_for_other(panels, direct, turned)
    theirs = lax.ppermute(other, AXES, TO_OTHER_CORE)
    mine, owned = product_for_me(panels, left)
    product = mine + theirs
    potential_blocks = owned.reshape(4, 1, 2, 1, NB, NB)
    return potential_blocks, jnp.swapaxes(product, 1, 2).reshape(2, 1, NB, 2, NB)


def solution(mesh):
    placed = (
        P(AXES, None, None, None),
        P(AXES, None),
        P(AXES),
        P(AXES, None, None),
        P(None, "dom", None, "col", None),
    )
    return jax.shard_map(
        shards,
        mesh=mesh,
        in_specs=placed,
        out_specs=(P(None, "dom", None, "col", None, None), P(None, "col", None, "dom", None)),
        check_vma=False,
    )
```
